32 devices in a mesh: ex: 8 (over z, x), tp: 4 (over y, core).
Axes of the slice: x: 2, y: 2, z: 4, core: 2. Of those that a mesh axis runs over, the one named last changes fastest.
Arguments:
- inputs: bfloat16 [1024, 768], P('ex'), may hold values from -6 to 6
- routes: int32 [1024, 2], P('ex'), may hold values from 0 to 7, all different within a row; in each aligned block of 128 rows (0 to 127, 128 to 255, ...) at most 64 rows name the same one
- lengths: int32 [8, 4], P('ex'), may hold values from 1 to 96, 128 in all within a row
- w_query: bfloat16 [768, 768], P(None, 'tp'), may hold values from -0.21875 to 0.21875
- w_key: bfloat16 [768, 768], P(None, 'tp'), may hold values from -0.21875 to 0.21875
- w_value: bfloat16 [768, 768], P(None, 'tp'), may hold values from -0.21875 to 0.21875
- w_attn_out: bfloat16 [768, 768], P('tp'), may hold values from -0.875 to 0.875
- gain_attn: float32 [768], replicated, may hold values from 0.25 to 1.75
- gain_moe: float32 [768], replicated, may hold values from 0.25 to 1.75
- rel_bias: float32 [32, 12], P(None, 'tp'), may hold values from -4 to 4
- w_router: bfloat16 [768, 8], replicated, may hold values from -0.15625 to 0.15625
- w_in: bfloat16 [8, 768, 3072], P('ex', None, 'tp'), may hold values from -0.21875 to 0.21875
- w_out: bfloat16 [8, 3072, 768], P('ex', 'tp'), may hold values from -0.109375 to 0.109375
- cotangent: bfloat16 [1024, 768], P('ex'), may hold values from -6 to 6
Outputs:
- output: bfloat16 [1024, 768], P('ex')
- grad_inputs: bfloat16 [1024, 768], P('ex')
- grad_w_query: float32 [768, 768], P(None, 'tp')
- grad_w_key: float32 [768, 768], P(None, 'tp')
- grad_w_value: float32 [768, 768], P(None, 'tp')
- grad_w_attn_out: float32 [768, 768], P('tp')
- grad_gain_attn: float32 [768], replicated
- grad_gain_moe: float32 [768], replicated
- grad_rel_bias: float32 [32, 12], P(None, 'tp')
- grad_w_router: float32 [768, 8], replicated
- grad_w_in: float32 [8, 768, 3072], P('ex', None, 'tp')
- grad_w_out: float32 [8, 3072, 768], P('ex', 'tp')
The draws below stay inside these ranges and needn't reach their ends.
Inputs may be any that keep to these rules, and one draw needn't show every extreme that they name: `routes`: each row names two different experts. The rows of one index of ex name any one expert at most 64 times, a bound that some block reaches. `lengths`: each row sums to 128 and its largest entry is exactly 96.
All inputs are finite; a program needn't handle non-finite values.
Results may differ from the reference program's by a relative error of at most 0.017.
Values may be sent and summed in bfloat16 or wider, within the bound.
A program may use at most 128 MiB of HBM per device.

```python
import math
import jax
import jax.numpy as jnp
import numpy as np
from jax import lax

D = 768
HEADS = 12
HEAD_DIM = 64
FF = 3072
BUCKETS = 32
SEQS_DEV = 4
TOK_DEV = 128
EXPERTS = 8
SEQ_MAX = 96
CAP = 64
TOKENS = 1024
SEQ_GROUPS = 8


def shard_levels(own_key, shape, split, smallest, largest):
    level = 1.0
    for dim, shards_of in split:
        heights = jax.random.uniform(jax.random.fold_in(jax.random.fold_in(own_key, 6), dim), (shards_of,), jnp.float32, smallest / len(split), largest / len(split))
        level = level * jnp.repeat(jnp.exp(heights), shape[dim] // shards_of).reshape((-1,) + (1,) * (len(shape) - 1 - dim))
    return level


def split_up(amount, total, bound, slope):
    loads = [(1 << 20) // math.isqrt(rank ** slope) + 1 for rank in range(2, amount + 1)]
    surplus, given = total - bound - (amount - 1), [1] * (amount - 1)
    while surplus > 0:
        movable = [i for i in range(amount - 1) if given[i] < bound]
        mass, left = sum([loads[i] for i in movable]), surplus
        for i in movable:
            extra = min(bound - given[i], max(1, left * loads[i] // mass), surplus)
            given[i] = given[i] + extra
            surplus = surplus - extra
    return np.array([bound] + given)


def uneven_parts(key, amount, total, most, slope):
    if amount == 2:
        one = jax.random.randint(key, (), max(1, total - most), min(most, total - 1) + 1)
        return jnp.stack([one, total - one])
    sizes = jnp.asarray(split_up(amount, total, most, slope), jnp.int32)
    pairs = (amount - 1) // 2
    source_of, taker = sizes[1:1 + 2 * pairs:2], sizes[2:2 + 2 * pairs:2]
    margin = jnp.minimum(source_of - 1, most - taker)
    passed = jax.random.randint(jax.random.fold_in(key, 1), (pairs,), 0, 1 << 20) % (margin + 1)
    sizes = sizes.at[1:1 + 2 * pairs:2].set(source_of - passed).at[2:2 + 2 * pairs:2].set(taker + passed)
    return sizes[jax.random.permutation(jax.random.fold_in(key, 2), amount)]


def assign_block(rng, own, number, rows, count, top, reach, lean):
    sequence = jax.random.permutation(rng, count)
    crowded, usual = shares(count, rows * top, reach, lean, True), shares(count, rows * top, reach, lean, False)
    places = jnp.arange(count)

    def named(tallies, rotation):
        used = int((tallies > 0).sum())
        fixed = max(1, used // 4)
        shifted = fixed + (places - fixed + rotation * (used - fixed)) % max(1, count - fixed)
        return jnp.zeros((count,), jnp.int32).at[sequence[jnp.where(places < fixed, places, shifted)]].set(jnp.asarray(tallies, jnp.int32))

    tallies = jnp.where(number % 4 == 0, named(crowded, number // 4), named(usual, number - number // 4 - 1))
    mixed = jax.random.permutation(jax.random.fold_in(own, 3), count)
    giver, sink = mixed[0:count // 2 * 2:2], mixed[1:count // 2 * 2:2]
    margin = jnp.minimum(tallies[giver] - 1, reach - tallies[sink]) // 2
    margin = jnp.where((giver == sequence[0]) | (sink == sequence[0]) | (tallies[sink] == 0), 0, jnp.maximum(margin, 0))
    shifted = jax.random.randint(jax.random.fold_in(own, 4), (count // 2,), 0, 1 << 20) % (margin + 1)
    tallies = tallies.at[giver].add(-shifted).at[sink].add(shifted)
    labels = jnp.searchsorted(jnp.cumsum(tallies), jnp.arange(rows * top), side="right").astype(jnp.int32)
    grid = labels.reshape(top, rows).T
    grid = grid[jax.random.permutation(jax.random.fold_in(own, 1), rows)]
    rotation = jax.random.randint(jax.random.fold_in(own, 2), (rows, 1), 0, top)
    return jnp.take_along_axis(grid, (jnp.arange(top)[None, :] + rotation) % top, axis=1)


def shares(amount, total, limit, skew, full):
    weights = [(1 << 20) // math.isqrt(rank ** skew) + 1 for rank in range(1, amount + 1)]
    largest = limit if full else min(limit, max(-(-total // amount), total * weights[0] // sum(weights)))
    least = 1 if total - largest >= amount - 1 else 0
    given, rest = [largest] + [least] * (amount - 1), total - largest - least * (amount - 1)
    while rest > 0:
        candidates = [i for i in range(1, amount) if given[i] < largest] or [i for i in range(1, amount) if given[i] < limit]
        mass, budget = sum([weights[i] for i in candidates]), rest
        for i in candidates:
            extra = min(limit - given[i], max(1, budget * weights[i] // mass), rest)
            given[i] = given[i] + extra
            rest = rest - extra
    return np.array(given)


def centred(rng, dims, deviation, bound, cuts=(), kind=jnp.bfloat16):
    values = deviation * jax.random.normal(rng, dims, jnp.float32)
    if cuts:
        values = values * shard_levels(rng, dims, cuts, -0.22, 0.18)
    return jnp.clip(values, -bound, bound).astype(kind)


def setup_inputs(seed: int = 0) -> dict:
    arg_keys = jax.random.split(jax.random.key(seed), 15)
    inputs = centred(arg_keys[0], (TOKENS, D), 1.0, 6.0, ((0, 8),))
    routes_keys = jax.random.split(jax.random.fold_in(arg_keys[1], 1), TOKENS // TOK_DEV)
    routes_turns = jax.random.permutation(jax.random.fold_in(arg_keys[1], 3), TOKENS // TOK_DEV)
    routes = jax.vmap(lambda own, number: assign_block(jax.random.fold_in(arg_keys[1], 2), own, number, TOK_DEV, EXPERTS, 2, CAP, 1))(routes_keys, routes_turns).reshape((TOKENS, 2))
    lengths = jax.vmap(lambda own: uneven_parts(own, SEQS_DEV, TOK_DEV, SEQ_MAX, 2))(jax.random.split(arg_keys[2], SEQ_GROUPS)).reshape((SEQ_GROUPS, SEQS_DEV)).astype(jnp.int32)
    w_query = centred(arg_keys[3], (D, D), D ** -0.5, 0.21875, ((1, 4),))
    w_key = centred(arg_keys[4], (D, D), D ** -0.5, 0.21875, ((1, 4),))
    w_value = centred(arg_keys[5], (D, D), D ** -0.5, 0.21875, ((1, 4),))
    w_attn_out = centred(arg_keys[6], (D, D), (D // 16) ** -0.5, 0.875, ((0, 4),))
    gain_attn = jnp.clip(1.0 + 0.15 * jax.random.normal(arg_keys[7], (D,), jnp.float32), 0.25, 1.75)
    gain_moe = jnp.clip(1.0 + 0.15 * jax.random.normal(arg_keys[8], (D,), jnp.float32), 0.25, 1.75)
    rel_bias = centred(arg_keys[9], (BUCKETS, HEADS), 1.0, 4.0, ((1, 4),), jnp.float32)
    w_router = centred(arg_keys[10], (D, EXPERTS), (2 * D) ** -0.5, 0.15625)
    w_in = centred(arg_keys[11], (EXPERTS, D, FF), D ** -0.5, 0.21875, ((0, 8), (2, 4)))
    w_out = centred(arg_keys[12], (EXPERTS, FF, D), FF ** -0.5, 0.109375, ((0, 8), (1, 4)))
    cotangent = centred(arg_keys[13], (TOKENS, D), 1.0, 6.0, ((0, 8),))
    return dict(inputs=inputs, routes=routes, lengths=lengths, w_query=w_query, w_key=w_key, w_value=w_value, w_attn_out=w_attn_out, gain_attn=gain_attn, gain_moe=gain_moe, rel_bias=rel_bias, w_router=w_router, w_in=w_in, w_out=w_out, cotangent=cotangent)


@jax.custom_vjp
def low(v):
    return lax.optimization_barrier(v.astype(jnp.bfloat16)).astype(jnp.float32)

@jax.custom_vjp
def low_back(v):
    return v

def low_keep(v):
    return (low(v), None)

def low_pass(kept, grad):
    return (grad,)

def back_keep(v):
    return (v, None)

def back_low(kept, grad):
    return (low(grad),)
low.defvjp(low_keep, low_pass)
low_back.defvjp(back_keep, back_low)
eps = 1e-06
highest = lax.Precision.HIGHEST
bucket_edges = [math.ceil(16 * 8 ** (number / 16)) for number in range(1, 16)]

def rms_scale(values):
    return lax.rsqrt(lax.optimization_barrier(jnp.mean(values * values, -1, keepdims=True)) + eps)

def bucket_of(length):
    positions = jnp.arange(length, dtype=jnp.int32)
    offsets = positions[:, None] - positions[None, :]
    distance = jnp.maximum(offsets, 0)
    counted = jnp.zeros_like(distance)
    for border in bucket_edges:
        counted = counted + (distance >= border).astype(jnp.int32)
    return jnp.where(distance < 16, distance, 16 + counted).astype(jnp.int32)

def segment_row(lengths_row):
    seq_ends = jnp.cumsum(lengths_row).astype(jnp.int32)
    positions = jnp.arange(TOK_DEV, dtype=jnp.int32)
    return lax.optimization_barrier(jnp.sum((positions[:, None] >= seq_ends[None, :]).astype(jnp.int32), -1)).astype(jnp.int32)

def reference(inputs, routes, lengths, w_query, w_key, w_value, w_attn_out, gain_attn, gain_moe, rel_bias, w_router, w_in, w_out, cotangent):
    attn_scale = HEAD_DIM ** (-0.5)
    buckets = bucket_of(TOK_DEV)
    one_hot = (buckets[None] == jnp.arange(BUCKETS, dtype=jnp.int32)[:, None, None]).astype(jnp.float32)
    positions = jnp.arange(TOK_DEV, dtype=jnp.int32)
    causal = positions[:, None] >= positions[None, :]
    segments = jax.vmap(segment_row)(lengths)
    allowed = (segments[:, :, None] == segments[:, None, :]) & causal[None]
    expert_ids = jnp.arange(EXPERTS, dtype=jnp.int32)
    pair_routes = routes.reshape(SEQ_GROUPS, 2 * TOK_DEV)
    chosen = (pair_routes[:, :, None] == expert_ids[None, None, :]).astype(jnp.int32)
    running = jnp.cumsum(chosen, axis=1).astype(jnp.int32)
    slot_index = (lax.optimization_barrier(jnp.sum(chosen * running, -1)) - 1).astype(jnp.int32)
    column = (jnp.arange(SEQ_GROUPS, dtype=jnp.int32)[:, None] * CAP + slot_index).astype(jnp.int32)
    pair_ids = jnp.arange(SEQ_GROUPS * 2 * TOK_DEV, dtype=jnp.int32).reshape(SEQ_GROUPS, 2 * TOK_DEV)
    slot_table = jnp.full((EXPERTS, SEQ_GROUPS * CAP), 2 * TOKENS, jnp.int32).at[pair_routes, column].set(pair_ids)
    route_hot = (routes[:, :, None] == expert_ids[None, None, :]).astype(jnp.float32)

    def forward(inputs_f, query_w, key_w, value_w, attn_out_w, attn_gain, moe_gain, bias_table, router_w, in_w, out_w):
        normed_a = inputs_f * rms_scale(inputs_f)
        attn_in = low(normed_a * attn_gain)
        query_f = low(low_back(jnp.dot(attn_in, query_w, precision=highest)))
        key_f = low(low_back(jnp.dot(attn_in, key_w, precision=highest)))
        value_f = low(low_back(jnp.dot(attn_in, value_w, precision=highest)))
        bias_full = jnp.einsum('bij,bh->hij', one_hot, bias_table, precision=highest)
        heads_q = query_f.reshape(SEQ_GROUPS, TOK_DEV, HEADS, HEAD_DIM)
        heads_k = key_f.reshape(SEQ_GROUPS, TOK_DEV, HEADS, HEAD_DIM)
        heads_v = value_f.reshape(SEQ_GROUPS, TOK_DEV, HEADS, HEAD_DIM)

        def attend(block_args):
            query_b, key_b, value_b, allowed_b = block_args
            raw_scores = low_back(jnp.einsum('ihd,jhd->hij', query_b, key_b, precision=highest) * attn_scale)
            scores = jnp.where(allowed_b[None], raw_scores + bias_full, -1e+30)
            row_max = lax.optimization_barrier(jnp.max(scores, -1, keepdims=True))
            weights = jnp.exp(scores - row_max)
            probabilities = weights / lax.optimization_barrier(jnp.sum(weights, -1, keepdims=True))
            return low(low_back(jnp.einsum('hij,jhd->ihd', low(probabilities), value_b, precision=highest)))
        mixed_heads = lax.map(jax.checkpoint(attend), (heads_q, heads_k, heads_v, allowed)).reshape(TOKENS, D)
        residual = inputs_f + low_back(jnp.dot(mixed_heads, attn_out_w, precision=highest))
        normed_m = residual * rms_scale(residual)
        moe_in = low(normed_m * moe_gain)
        logits = jnp.dot(moe_in, router_w, precision=highest)
        chosen_logits = lax.optimization_barrier(jnp.sum(route_hot * logits[:, None, :], -1))
        gate_max = lax.optimization_barrier(jnp.max(chosen_logits, -1, keepdims=True))
        gate_exp = jnp.exp(chosen_logits - gate_max)
        gate_values = gate_exp / lax.optimization_barrier(jnp.sum(gate_exp, -1, keepdims=True))
        padded = jnp.concatenate([moe_in, jnp.zeros((1, D), jnp.float32)], 0)

        def expert(block_args):
            weight_in, weight_out, members = block_args
            rows_in = low_back(padded[members // 2])
            pre_act = low_back(jnp.dot(rows_in, weight_in, precision=highest))
            act_low = low(jax.nn.gelu(pre_act, approximate=True))
            return low(low_back(jnp.dot(act_low, weight_out, precision=highest)))
        expert_out = lax.map(jax.checkpoint(expert), (in_w, out_w, slot_table))
        per_pair = jnp.zeros((2 * TOKENS + 1, D), jnp.float32).at[slot_table.reshape(-1)].add(expert_out.reshape(-1, D))
        per_pair = per_pair[:2 * TOKENS].reshape(TOKENS, 2, D)
        return residual + lax.optimization_barrier(jnp.sum(gate_values[:, :, None] * per_pair, 1))
    arrays = (inputs.astype(jnp.float32), w_query.astype(jnp.float32), w_key.astype(jnp.float32), w_value.astype(jnp.float32), w_attn_out.astype(jnp.float32), gain_attn, gain_moe, rel_bias, w_router.astype(jnp.float32), w_in.astype(jnp.float32), w_out.astype(jnp.float32))
    result, pullback = jax.vjp(forward, *arrays)
    gradients = pullback(cotangent.astype(jnp.float32))
    return (result.astype(jnp.bfloat16), gradients[0].astype(jnp.bfloat16), gradients[1], gradients[2], gradients[3], gradients[4], gradients[5], gradients[6], gradients[7], gradients[8], gradients[9], gradients[10])
```

```python
from functools import partial
import math

import jax
import jax.numpy as jnp
from jax import lax
from jax.sharding import PartitionSpec as P

eps = 1e-06
highest = lax.Precision.HIGHEST
bucket_edges = [math.ceil(16 * 8 ** (number / 16)) for number in range(1, 16)]


def rms_scale(values):
    return lax.rsqrt(jnp.mean(values * values, -1, keepdims=True) + eps)


def bucket_of(length):
    positions = jnp.arange(length, dtype=jnp.int32)
    offsets = positions[:, None] - positions[None, :]
    distance = jnp.maximum(offsets, 0)
    counted = jnp.zeros_like(distance)
    for border in bucket_edges:
        counted = counted + (distance >= border).astype(jnp.int32)
    return jnp.where(distance < 16, distance, 16 + counted)


def contract_rows(left_side, right_side):
    return lax.dot_general(
        left_side, right_side, (((0,), (0,)), ((), ())), preferred_element_type=jnp.float32
    )


def contract_cols(left_side, right_side):
    return lax.dot_general(
        left_side, right_side, (((1,), (1,)), ((), ())), preferred_element_type=jnp.float32
    )


def shards(
    inputs,
    routes,
    lengths,
    w_query,
    w_key,
    w_value,
    w_attn_out,
    gain_attn,
    gain_moe,
    rel_bias,
    w_router,
    w_in,
    w_out,
    cotangent,
):
    tok_rows, model_width = inputs.shape
    local_heads = rel_bias.shape[1]
    head_dim = w_query.shape[1] // local_heads
    attn_scale = head_dim ** (-0.5)
    experts = w_router.shape[1]
    ex_devices = lax.axis_size("ex")
    local_experts = w_in.shape[0]
    capacity = 4 * tok_rows // experts
    pair_count = 2 * tok_rows
    inputs_f = inputs.astype(jnp.float32)
    scale_a = rms_scale(inputs_f)
    normed_a = inputs_f * scale_a
    attn_in = (normed_a * gain_attn).astype(jnp.bfloat16)
    query_b = (
        jnp.dot(attn_in, w_query, preferred_element_type=jnp.float32)
        .astype(jnp.bfloat16)
        .reshape(tok_rows, local_heads, head_dim)
    )
    key_b = (
        jnp.dot(attn_in, w_key, preferred_element_type=jnp.float32)
        .astype(jnp.bfloat16)
        .reshape(tok_rows, local_heads, head_dim)
    )
    value_b = (
        jnp.dot(attn_in, w_value, preferred_element_type=jnp.float32)
        .astype(jnp.bfloat16)
        .reshape(tok_rows, local_heads, head_dim)
    )
    buckets = bucket_of(tok_rows)
    one_hot = (
        buckets[None] == jnp.arange(rel_bias.shape[0], dtype=jnp.int32)[:, None, None]
    ).astype(jnp.float32)
    bias_full = jnp.einsum("bij,bh->hij", one_hot, rel_bias, precision=highest)
    seq_count = lengths.shape[1]
    seq_order = jnp.arange(seq_count, dtype=jnp.int32)
    seq_ends = jnp.sum(
        jnp.where(seq_order[None, :] <= seq_order[:, None], lengths[0][None, :], 0), -1
    )
    positions = jnp.arange(tok_rows, dtype=jnp.int32)
    segments = jnp.sum((positions[:, None] >= seq_ends[None, :]).astype(jnp.int32), -1)
    allowed = (segments[:, None] == segments[None, :]) & (positions[:, None] >= positions[None, :])

    def score_of(queries_in, keys_in):
        raw_scores = (
            jnp.einsum("ihd,jhd->hij", queries_in, keys_in, preferred_element_type=jnp.float32)
            * attn_scale
        )
        return jnp.where(allowed[None], raw_scores + bias_full, -1e30)

    scores = score_of(query_b, key_b)
    row_max = jnp.max(scores, -1, keepdims=True)
    log_sum = row_max + jnp.log(jnp.sum(jnp.exp(scores - row_max), -1, keepdims=True))
    probabilities = jnp.exp(scores - log_sum)
    probs_low = probabilities.astype(jnp.bfloat16)
    mixed_heads = (
        jnp.einsum("hij,jhd->ihd", probs_low, value_b, preferred_element_type=jnp.float32)
        .astype(jnp.bfloat16)
        .reshape(tok_rows, -1)
    )
    head_part = jnp.dot(mixed_heads, w_attn_out, preferred_element_type=jnp.float32)
    residual = inputs_f + lax.psum(head_part, "tp")
    scale_m = rms_scale(residual)
    normed_m = residual * scale_m
    moe_in = (normed_m * gain_moe).astype(jnp.bfloat16)
    logits = jnp.dot(moe_in, w_router, preferred_element_type=jnp.float32)
    expert_ids = jnp.arange(experts, dtype=jnp.int32)
    route_hot = (routes[:, :, None] == expert_ids[None, None, :]).astype(jnp.float32)
    chosen_logits = jnp.sum(route_hot * logits[:, None, :], -1)
    gate_max = jnp.max(chosen_logits, -1, keepdims=True)
    gate_exp = jnp.exp(chosen_logits - gate_max)
    gate_values = gate_exp / jnp.sum(gate_exp, -1, keepdims=True)
    pair_routes = routes.reshape(-1)
    pair_hot = (pair_routes[:, None] == expert_ids[None, :]).astype(jnp.int32)
    pair_order = jnp.arange(pair_count, dtype=jnp.int32)
    slot_index = jnp.sum(
        (
            (pair_routes[:, None] == pair_routes[None, :])
            & (pair_order[None, :] < pair_order[:, None])
        ).astype(jnp.int32),
        -1,
    )
    pair_slots = pair_routes * capacity + slot_index
    members = (
        jnp.full((experts * capacity,), pair_count, jnp.int32)
        .at[pair_slots]
        .set(jnp.arange(pair_count, dtype=jnp.int32))
    )
    padded = jnp.concatenate([moe_in, jnp.zeros((1, model_width), jnp.bfloat16)], 0)
    send_rows = padded[members // 2].reshape(experts, capacity, model_width)
    arrived = lax.all_to_all(send_rows, "ex", split_axis=0, concat_axis=0, tiled=True)
    slot_count = arrived.shape[1]
    grouped = arrived.reshape(ex_devices, local_experts, slot_count, model_width)
    pre_act = jnp.einsum("slcd,ldf->slcf", grouped, w_in, preferred_element_type=jnp.float32)
    act_low = jax.nn.gelu(pre_act, approximate=True).astype(jnp.bfloat16)
    partial_out = jnp.einsum("slcf,lfd->slcd", act_low, w_out, preferred_element_type=jnp.float32)
    partial_out = partial_out.reshape(ex_devices * local_experts, slot_count, model_width)
    owned_rows = lax.psum_scatter(
        partial_out.astype(jnp.bfloat16), "tp", scatter_dimension=2, tiled=True
    )
    returned = lax.all_to_all(owned_rows, "ex", split_axis=0, concat_axis=0, tiled=True)
    returned, kept_rows, kept_pre = (
        returned,
        arrived,
        pre_act.reshape(ex_devices * local_experts, slot_count, -1),
    )
    expert_out = lax.all_gather(returned, "tp", axis=2, tiled=True).reshape(
        experts * capacity, model_width
    )
    pair_out = expert_out[pair_slots].reshape(tok_rows, 2, model_width).astype(jnp.float32)
    result = residual + jnp.sum(gate_values[:, :, None] * pair_out, 1)
    output = result.astype(jnp.bfloat16)
    grad_out = cotangent.astype(jnp.float32)
    gate_grad = jnp.sum(grad_out[:, None, :] * pair_out, -1)
    logit_pair = gate_values * (gate_grad - jnp.sum(gate_values * gate_grad, -1, keepdims=True))
    logit_grads = jnp.sum(logit_pair[:, :, None] * route_hot, 1)
    grad_router = jnp.dot(moe_in.astype(jnp.float32).T, logit_grads, precision=highest)
    moe_grad = jnp.dot(logit_grads, w_router.astype(jnp.float32).T, precision=highest)
    pair_grads = (
        (gate_values[:, :, None] * grad_out[:, None, :])
        .astype(jnp.bfloat16)
        .reshape(pair_count, model_width)
    )
    padded_grads = jnp.concatenate([pair_grads, jnp.zeros((1, model_width), jnp.bfloat16)], 0)
    send_grad_rows = padded_grads[members].reshape(experts, capacity, model_width)
    arrived_grads = lax.all_to_all(send_grad_rows, "ex", split_axis=0, concat_axis=0, tiled=True)
    grad_group = arrived_grads.reshape(ex_devices, local_experts, capacity, model_width)
    act_grad = jnp.einsum("slcd,lfd->slcf", grad_group, w_out, preferred_element_type=jnp.float32)
    pre_keep = kept_pre.reshape(ex_devices, local_experts, capacity, -1)
    act_value, gelu_back = jax.vjp(partial(jax.nn.gelu, approximate=True), pre_keep)
    pre_grad = gelu_back(act_grad)[0].astype(jnp.bfloat16)
    act_low = act_value.astype(jnp.bfloat16)
    grad_w_out = jnp.einsum(
        "slcf,slcd->lfd", act_low, grad_group, preferred_element_type=jnp.float32
    )
    rows_group = kept_rows.reshape(ex_devices, local_experts, capacity, model_width)
    grad_w_in = jnp.einsum(
        "slcd,slcf->ldf", rows_group, pre_grad, preferred_element_type=jnp.float32
    )
    row_part = jnp.einsum("slcf,ldf->slcd", pre_grad, w_in, preferred_element_type=jnp.float32)
    row_part = row_part.reshape(ex_devices * local_experts, capacity, model_width)
    row_share = lax.psum_scatter(row_part, "tp", scatter_dimension=2, tiled=True).astype(
        jnp.bfloat16
    )
    row_back = lax.all_to_all(row_share, "ex", split_axis=0, concat_axis=0, tiled=True)
    row_full = lax.all_gather(row_back, "tp", axis=2, tiled=True).reshape(
        experts * capacity, model_width
    )
    moe_grad = moe_grad + jnp.sum(
        row_full[pair_slots].reshape(tok_rows, 2, model_width).astype(jnp.float32), 1
    )
    grad_gain_moe = jnp.sum(moe_grad * normed_m, 0)
    normed_grad_m = moe_grad * gain_moe
    resid_grad = grad_out + scale_m * (
        normed_grad_m - normed_m * jnp.mean(normed_grad_m * normed_m, -1, keepdims=True)
    )
    attn_grad = resid_grad.astype(jnp.bfloat16)
    grad_w_attn_out = contract_rows(mixed_heads, attn_grad)
    mixed_grad = (
        contract_cols(attn_grad, w_attn_out)
        .astype(jnp.bfloat16)
        .reshape(tok_rows, local_heads, head_dim)
    )
    scores_again = score_of(query_b, key_b)
    probs_again = jnp.exp(scores_again - log_sum)
    prob_grad = jnp.einsum("ihd,jhd->hij", mixed_grad, value_b, preferred_element_type=jnp.float32)
    value_grad = jnp.einsum(
        "hij,ihd->jhd",
        probs_again.astype(jnp.bfloat16),
        mixed_grad,
        preferred_element_type=jnp.float32,
    ).astype(jnp.bfloat16)
    score_grad = probs_again * (prob_grad - jnp.sum(probs_again * prob_grad, -1, keepdims=True))
    grad_rel_bias = jnp.einsum("hij,bij->bh", score_grad, one_hot, precision=highest)
    score_low = score_grad.astype(jnp.bfloat16)
    query_grad = (
        (
            jnp.einsum("hij,jhd->ihd", score_low, key_b, preferred_element_type=jnp.float32)
            * attn_scale
        )
        .astype(jnp.bfloat16)
        .reshape(tok_rows, -1)
    )
    key_grad = (
        (
            jnp.einsum("hij,ihd->jhd", score_low, query_b, preferred_element_type=jnp.float32)
            * attn_scale
        )
        .astype(jnp.bfloat16)
        .reshape(tok_rows, -1)
    )
    value_flat = value_grad.reshape(tok_rows, -1)
    grad_w_query = contract_rows(attn_in, query_grad)
    grad_w_key = contract_rows(attn_in, key_grad)
    grad_w_value = contract_rows(attn_in, value_flat)
    input_part = (
        contract_cols(query_grad, w_query)
        + contract_cols(key_grad, w_key)
        + contract_cols(value_flat, w_value)
    )
    input_grad = lax.psum(input_part.astype(jnp.bfloat16), "tp").astype(jnp.float32)
    grad_gain_attn = jnp.sum(input_grad * normed_a, 0)
    normed_grad_a = input_grad * gain_attn
    grad_inputs = (
        resid_grad
        + scale_a
        * (normed_grad_a - normed_a * jnp.mean(normed_grad_a * normed_a, -1, keepdims=True))
    ).astype(jnp.bfloat16)
    dense_sums = lax.psum(
        (
            grad_w_query,
            grad_w_key,
            grad_w_value,
            grad_w_attn_out,
            grad_gain_attn,
            grad_gain_moe,
            grad_rel_bias,
            grad_router,
        ),
        "ex",
    )
    return (
        output,
        grad_inputs,
        dense_sums[0],
        dense_sums[1],
        dense_sums[2],
        dense_sums[3],
        dense_sums[4],
        dense_sums[5],
        dense_sums[6],
        dense_sums[7],
        grad_w_in,
        grad_w_out,
    )


def solution(mesh):
    placed = (
        P("ex", None),
        P("ex", None),
        P("ex", None),
        P(None, "tp"),
        P(None, "tp"),
        P(None, "tp"),
        P("tp", None),
        P(),
        P(),
        P(None, "tp"),
        P(),
        P("ex", None, "tp"),
        P("ex", "tp", None),
        P("ex", None),
    )
    return jax.shard_map(
        shards,
        mesh=mesh,
        in_specs=placed,
        out_specs=(
            P("ex", None),
            P("ex", None),
            P(None, "tp"),
            P(None, "tp"),
            P(None, "tp"),
            P("tp", None),
            P(),
            P(),
            P(None, "tp"),
            P(),
            P("ex", None, "tp"),
            P("ex", "tp", None),
        ),
        check_vma=False,
    )
```

```python
from functools import partial
import math

import jax
import jax.numpy as jnp
from jax import lax
from jax.experimental import pallas as pl
from jax.experimental.pallas import tpu as pltpu
from jax.sharding import PartitionSpec as P

eps = 1e-06
highest = lax.Precision.HIGHEST
bucket_edges = [math.ceil(16 * 8 ** (number / 16)) for number in range(1, 16)]


def rms_scale(values):
    return lax.rsqrt(jnp.mean(values * values, -1, keepdims=True) + eps)


def bucket_of(length):
    positions = jnp.arange(length, dtype=jnp.int32)
    offsets = positions[:, None] - positions[None, :]
    distance = jnp.maximum(offsets, 0)
    counted = jnp.zeros_like(distance)
    for border in bucket_edges:
        counted = counted + (distance >= border).astype(jnp.int32)
    return jnp.where(distance < 16, distance, 16 + counted)


def contract_rows(left_side, right_side):
    return lax.dot_general(
        left_side, right_side, (((0,), (0,)), ((), ())), preferred_element_type=jnp.float32
    )


def contract_cols(left_side, right_side):
    return lax.dot_general(
        left_side, right_side, (((1,), (1,)), ((), ())), preferred_element_type=jnp.float32
    )


VMEM_BYTES = 48 * 2**20


def flip(index, bit):
    return index + bit * (1 - 2 * ((index // bit) % 2))


def flip_all(index, offset):
    bit = 1
    while bit <= offset:
        if offset & bit:
            index = flip(index, bit)
        bit *= 2
    return index


def bits_of(count):
    bits = []
    bit = count // 2
    while bit:
        bits.append(bit)
        bit //= 2
    return bits


def remote(src, dst, send_sem, recv_sem, axis, peer):
    return pltpu.make_async_remote_copy(
        src_ref=src,
        dst_ref=dst,
        send_sem=send_sem,
        recv_sem=recv_sem,
        device_id={axis: peer},
        device_id_type=pl.DeviceIdType.MESH,
    )


def greet(partners):
    barrier = pltpu.get_barrier_semaphore()
    for axis, peer in partners:
        pl.semaphore_signal(
            barrier, inc=1, device_id={axis: peer}, device_id_type=pl.DeviceIdType.MESH
        )
    pl.semaphore_wait(barrier, len(partners))


def all_peers(axis, count):
    me = lax.axis_index(axis)
    return [(axis, lax.rem(me + step, count)) for step in range(1, count)]


def bit_peers(axis, count):
    me = lax.axis_index(axis)
    return [(axis, flip(me, bit)) for bit in bits_of(count)]


def double_gather(axis, count, sets):
    me = lax.axis_index(axis)
    bits = bits_of(count)
    sent = []

    def send(offset, stage):
        for bit in bits[stage:]:
            for view, send_sems, recv_sems in sets:
                block = view(flip_all(me, offset))
                copy = remote(
                    block,
                    block,
                    send_sems.at[offset ^ bit],
                    recv_sems.at[offset ^ bit],
                    axis,
                    flip(me, bit),
                )
                copy.start()
                sent.append(copy)

    send(0, 0)
    held = [0]
    for stage, bit in enumerate(bits):
        fresh = []
        for offset in held:
            arrived = offset ^ bit
            for view, send_sems, recv_sems in sets:
                block = view(flip_all(me, arrived))
                remote(
                    block, block, send_sems.at[arrived], recv_sems.at[arrived], axis, flip(me, bit)
                ).wait_recv()
            send(arrived, stage + 1)
            fresh.append(arrived)
        held = held + fresh
    return sent


def swap_blocks(axis, count, source, target, send_sems, recv_sems):
    me = lax.axis_index(axis)
    sent = []
    for step in range(1, count):
        peer = lax.rem(me + step, count)
        copy = remote(
            source(peer), target(me), send_sems.at[step], recv_sems.at[step], axis, peer
        )
        copy.start()
        sent.append(copy)
    for step in range(1, count):
        origin = lax.rem(me + count - step, count)
        remote(
            source(origin), target(origin), send_sems.at[step], recv_sems.at[step], axis, origin
        ).wait_recv()
    return sent


def finish(sent):
    for copy in sent:
        copy.wait_send()


def sum_kernel(axis, count, x_ref, out_ref, low_ref, got_ref, s1, r1, s2, r2):
    me = lax.axis_index(axis)
    rows = x_ref.shape[0] // count

    def part(ref, index):
        return ref.at[pl.ds(pl.multiple_of(index * rows, rows), rows)]

    low_ref[...] = x_ref[...].astype(jnp.bfloat16)
    greet(all_peers(axis, count))
    first = swap_blocks(
        axis, count, lambda i: part(low_ref, i), lambda i: got_ref.at[i], s1, r1
    )
    mine = pl.ds(pl.multiple_of(me * rows, rows), rows)
    got_ref[me] = jnp.zeros(got_ref.shape[1:], jnp.bfloat16)
    total = x_ref[mine, :].astype(jnp.float32)
    for index in range(count):
        total = total + got_ref[index].astype(jnp.float32)
    out_ref[mine, :] = total.astype(jnp.bfloat16)
    second = double_gather(axis, count, [(lambda i: part(out_ref, i), s2, r2)])
    finish(first + second)


def dispatch_kernel(ex, tp, x_ref, out_ref, s1, r1, s2, r2):
    me = lax.axis_index("ex")
    column = lax.axis_index("tp")
    greet(all_peers("ex", ex) + bit_peers("tp", tp))
    out_ref[column, me] = x_ref[me]
    first = swap_blocks(
        "ex", ex, lambda i: x_ref.at[i], lambda i: out_ref.at[column, i], s1, r1
    )
    second = double_gather("tp", tp, [(lambda i: out_ref.at[i], s2, r2)])
    finish(first + second)


def return_kernel(ex, tp, x_ref, out_ref, held_ref, got_ref, s1, r1, s2, r2):
    me = lax.axis_index("ex")
    column = lax.axis_index("tp")
    greet(all_peers("ex", ex) + bit_peers("tp", tp))
    sent = []
    live = list(range(tp))
    source = x_ref
    for bit in reversed(bits_of(tp)):
        leaving = [offset for offset in live if offset & bit]
        for offset in leaving:
            copy = remote(
                source.at[flip_all(column, offset)],
                got_ref.at[offset],
                s1.at[offset],
                r1.at[offset],
                "tp",
                flip(column, bit),
            )
            copy.start()
            sent.append(copy)
        for offset in leaving:
            kept = flip_all(column, offset ^ bit)
            remote(
                source.at[kept], got_ref.at[offset], s1.at[offset], r1.at[offset], "tp", flip(column, bit)
            ).wait_recv()
            held_ref[kept] = (
                source[kept].astype(jnp.float32) + got_ref[offset].astype(jnp.float32)
            ).astype(jnp.bfloat16)
        live = [offset for offset in live if not offset & bit]
        source = held_ref
    out_ref[me] = held_ref[column, me]
    second = swap_blocks(
        "ex", ex, lambda i: held_ref.at[column, i], lambda i: out_ref.at[i], s2, r2
    )
    finish(sent + second)


def gather_kernel(axis, count, number, *refs):
    me = lax.axis_index(axis)
    ins, outs, sems = refs[:number], refs[number : 2 * number], refs[2 * number :]
    greet(bit_peers(axis, count))
    sets = []
    for index in range(number):
        out_ref = outs[index]
        out_ref[me] = ins[index][...]
        sets.append(
            (lambda i, out_ref=out_ref: out_ref.at[i], sems[2 * index], sems[2 * index + 1])
        )
    finish(double_gather(axis, count, sets))


def call_kernel(body, ident, out_shapes, scratch, *operands):
    return pl.pallas_call(
        body,
        out_shape=out_shapes,
        in_specs=[pl.BlockSpec(memory_space=pltpu.VMEM)] * len(operands),
        out_specs=jax.tree.map(lambda _: pl.BlockSpec(memory_space=pltpu.VMEM), out_shapes),
        scratch_shapes=scratch,
        compiler_params=pltpu.CompilerParams(
            collective_id=ident, has_side_effects=True, vmem_limit_bytes=VMEM_BYTES
        ),
    )(*operands)


def sems(*counts):
    return [pltpu.SemaphoreType.DMA((count,)) for count in counts]


def low_shape(*shape):
    return jax.ShapeDtypeStruct(shape, jnp.bfloat16)


def sum_over_tp(values, ident):
    count = lax.axis_size("tp")
    rows, width = values.shape
    return call_kernel(
        partial(sum_kernel, "tp", count),
        ident,
        low_shape(rows, width),
        [
            pltpu.VMEM((rows, width), jnp.bfloat16),
            pltpu.VMEM((count, rows // count, width), jnp.bfloat16),
        ]
        + sems(count, count, count, count),
        values,
    )


def gather_blocks(axis, ident, *arrays):
    count = lax.axis_size(axis)
    return call_kernel(
        partial(gather_kernel, axis, count, len(arrays)),
        ident,
        [low_shape(count, *array.shape) for array in arrays],
        sems(*([count] * (2 * len(arrays)))),
        *arrays,
    )


def shards(
    inputs,
    routes,
    lengths,
    w_query,
    w_key,
    w_value,
    w_attn_out,
    gain_attn,
    gain_moe,
    rel_bias,
    w_router,
    w_in,
    w_out,
    cotangent,
):
    tok_rows, model_width = inputs.shape
    local_heads = rel_bias.shape[1]
    head_dim = w_query.shape[1] // local_heads
    attn_scale = head_dim ** (-0.5)
    experts = w_router.shape[1]
    ex_devices = lax.axis_size("ex")
    local_experts = w_in.shape[0]
    capacity = 4 * tok_rows // experts
    pair_count = 2 * tok_rows
    inputs_f = inputs.astype(jnp.float32)
    scale_a = rms_scale(inputs_f)
    normed_a = inputs_f * scale_a
    attn_in = (normed_a * gain_attn).astype(jnp.bfloat16)
    query_b = (
        jnp.dot(attn_in, w_query, preferred_element_type=jnp.float32)
        .astype(jnp.bfloat16)
        .reshape(tok_rows, local_heads, head_dim)
    )
    key_b = (
        jnp.dot(attn_in, w_key, preferred_element_type=jnp.float32)
        .astype(jnp.bfloat16)
        .reshape(tok_rows, local_heads, head_dim)
    )
    value_b = (
        jnp.dot(attn_in, w_value, preferred_element_type=jnp.float32)
        .astype(jnp.bfloat16)
        .reshape(tok_rows, local_heads, head_dim)
    )
    buckets = bucket_of(tok_rows)
    one_hot = (
        buckets[None] == jnp.arange(rel_bias.shape[0], dtype=jnp.int32)[:, None, None]
    ).astype(jnp.float32)
    bias_full = jnp.einsum("bij,bh->hij", one_hot, rel_bias, precision=highest)
    seq_count = lengths.shape[1]
    seq_order = jnp.arange(seq_count, dtype=jnp.int32)
    seq_ends = jnp.sum(
        jnp.where(seq_order[None, :] <= seq_order[:, None], lengths[0][None, :], 0), -1
    )
    positions = jnp.arange(tok_rows, dtype=jnp.int32)
    segments = jnp.sum((positions[:, None] >= seq_ends[None, :]).astype(jnp.int32), -1)
    allowed = (segments[:, None] == segments[None, :]) & (positions[:, None] >= positions[None, :])

    def score_of(queries_in, keys_in):
        raw_scores = (
            jnp.einsum("ihd,jhd->hij", queries_in, keys_in, preferred_element_type=jnp.float32)
            * attn_scale
        )
        return jnp.where(allowed[None], raw_scores + bias_full, -1e30)

    scores = score_of(query_b, key_b)
    row_max = jnp.max(scores, -1, keepdims=True)
    log_sum = row_max + jnp.log(jnp.sum(jnp.exp(scores - row_max), -1, keepdims=True))
    probabilities = jnp.exp(scores - log_sum)
    probs_low = probabilities.astype(jnp.bfloat16)
    mixed_heads = (
        jnp.einsum("hij,jhd->ihd", probs_low, value_b, preferred_element_type=jnp.float32)
        .astype(jnp.bfloat16)
        .reshape(tok_rows, -1)
    )
    all_attn_in = lax.all_gather(attn_in, "ex", axis=0, tiled=True)
    all_mixed = lax.all_gather(mixed_heads, "ex", axis=0, tiled=True)
    head_part = jnp.dot(mixed_heads, w_attn_out, preferred_element_type=jnp.float32)
    residual = inputs_f + sum_over_tp(head_part, 0).astype(jnp.float32)
    scale_m = rms_scale(residual)
    normed_m = residual * scale_m
    moe_in = (normed_m * gain_moe).astype(jnp.bfloat16)
    logits = jnp.dot(moe_in, w_router, preferred_element_type=jnp.float32)
    expert_ids = jnp.arange(experts, dtype=jnp.int32)
    route_hot = (routes[:, :, None] == expert_ids[None, None, :]).astype(jnp.float32)
    chosen_logits = jnp.sum(route_hot * logits[:, None, :], -1)
    gate_max = jnp.max(chosen_logits, -1, keepdims=True)
    gate_exp = jnp.exp(chosen_logits - gate_max)
    gate_values = gate_exp / jnp.sum(gate_exp, -1, keepdims=True)
    pair_routes = routes.reshape(-1)
    pair_hot = (pair_routes[:, None] == expert_ids[None, :]).astype(jnp.int32)
    pair_order = jnp.arange(pair_count, dtype=jnp.int32)
    slot_index = jnp.sum(
        (
            (pair_routes[:, None] == pair_routes[None, :])
            & (pair_order[None, :] < pair_order[:, None])
        ).astype(jnp.int32),
        -1,
    )
    pair_slots = pair_routes * capacity + slot_index
    slot_total = experts * capacity
    pair_cols = pair_slots.reshape(tok_rows, 2).T.reshape(1, pair_count)
    slot_hot = (
        jnp.arange(slot_total, dtype=jnp.int32)[:, None] == pair_cols
    ).astype(jnp.bfloat16)
    grad_out = cotangent.astype(jnp.float32)
    tp_devices = lax.axis_size("tp")
    tp_index = lax.axis_index("tp")
    share = 2 * model_width // tp_devices
    half = tp_devices // 2
    moe_pairs = jnp.concatenate([moe_in, moe_in], 0)
    grad_pairs = jnp.concatenate(
        [(gate_values[:, j : j + 1] * grad_out).astype(jnp.bfloat16) for j in range(2)], 0
    )
    pair_rows = lax.dynamic_slice_in_dim(
        jnp.concatenate([moe_pairs, grad_pairs], 1), tp_index * share, share, 1
    )
    send_rows = (
        jnp.dot(slot_hot, pair_rows, preferred_element_type=jnp.float32)
        .astype(jnp.bfloat16)
        .reshape(ex_devices, slot_total // ex_devices, share)
    )
    slots_here = slot_total // ex_devices
    arrived = call_kernel(
        partial(dispatch_kernel, ex_devices, tp_devices),
        1,
        low_shape(tp_devices, ex_devices, slots_here, share),
        sems(ex_devices, ex_devices, tp_devices, tp_devices),
        send_rows,
    ).reshape(tp_devices, slot_total, share)
    moe_rows = jnp.concatenate([arrived[i] for i in range(half)], 1)
    grad_rows = jnp.concatenate([arrived[i] for i in range(half, tp_devices)], 1)
    in_here, out_here = w_in[0], w_out[0]
    pre_act = jnp.dot(moe_rows, in_here, preferred_element_type=jnp.float32)
    act_value, gelu_back = jax.vjp(partial(jax.nn.gelu, approximate=True), pre_act)
    act_low = act_value.astype(jnp.bfloat16)
    act_grad = contract_cols(grad_rows, out_here)
    pre_grad = gelu_back(act_grad)[0].astype(jnp.bfloat16)
    partial_out = jnp.dot(act_low, out_here, preferred_element_type=jnp.float32)
    row_part = contract_cols(pre_grad, in_here)
    back_rows = jnp.stack(
        [
            block[:, i * share : (i + 1) * share].astype(jnp.bfloat16)
            for block in (partial_out, row_part)
            for i in range(half)
        ]
    ).reshape(tp_devices, ex_devices, slots_here, share)
    returned = call_kernel(
        partial(return_kernel, ex_devices, tp_devices),
        2,
        low_shape(ex_devices, slots_here, share),
        [
            pltpu.VMEM((tp_devices, ex_devices, slots_here, share), jnp.bfloat16),
            pltpu.VMEM((tp_devices, ex_devices, slots_here, share), jnp.bfloat16),
        ]
        + sems(tp_devices, tp_devices, ex_devices, ex_devices),
        back_rows,
    ).reshape(slot_total, share)
    grad_w_out = contract_rows(act_low, grad_rows)[None]
    grad_w_in = contract_rows(moe_rows, pre_grad)[None]
    pair_back = contract_rows(slot_hot, returned)
    is_out = tp_index < half
    weights = jnp.where(is_out, gate_values, 1.0)
    combined = (
        weights[:, 0:1] * pair_back[:tok_rows] + weights[:, 1:2] * pair_back[tok_rows:]
    )
    grad_cols = lax.dynamic_slice_in_dim(grad_out, (tp_index % half) * share, share, 1)
    gate_part = jnp.where(
        is_out,
        jnp.stack(
            [
                jnp.sum(grad_cols * pair_back[:tok_rows], -1),
                jnp.sum(grad_cols * pair_back[tok_rows:], -1),
            ],
            1,
        ),
        0.0,
    )
    gate_high = gate_part.astype(jnp.bfloat16)
    gate_low = (gate_part - gate_high.astype(jnp.float32)).astype(jnp.bfloat16)
    [shared] = gather_blocks(
        "tp",
        3,
        jnp.concatenate(
            [
                combined.astype(jnp.bfloat16),
                gate_high,
                gate_low,
                jnp.zeros((tok_rows, 124), jnp.bfloat16),
            ],
            1,
        ),
    )
    shared = shared.astype(jnp.float32)
    output = (
        residual + jnp.concatenate([shared[i, :, :share] for i in range(half)], 1)
    ).astype(jnp.bfloat16)
    row_sum = jnp.concatenate([shared[i, :, :share] for i in range(half, tp_devices)], 1)
    gate_grad = jnp.sum(
        shared[:, :, share : share + 2] + shared[:, :, share + 2 : share + 4], 0
    )
    logit_pair = gate_values * (gate_grad - jnp.sum(gate_values * gate_grad, -1, keepdims=True))
    logit_grads = jnp.sum(logit_pair[:, :, None] * route_hot, 1)
    router_rows = jnp.dot(logit_grads.T, moe_in.astype(jnp.float32), precision=highest)
    moe_grad = row_sum + jnp.dot(logit_grads, w_router.astype(jnp.float32).T, precision=highest)
    grad_gain_moe = jnp.sum(moe_grad * normed_m, 0)
    normed_grad_m = moe_grad * gain_moe
    resid_grad = grad_out + scale_m * (
        normed_grad_m - normed_m * jnp.mean(normed_grad_m * normed_m, -1, keepdims=True)
    )
    attn_grad = resid_grad.astype(jnp.bfloat16)
    all_attn_grad = lax.all_gather(attn_grad, "ex", axis=0, tiled=True)
    grad_w_attn_out = contract_rows(all_mixed, all_attn_grad)
    mixed_grad = (
        contract_cols(attn_grad, w_attn_out)
        .astype(jnp.bfloat16)
        .reshape(tok_rows, local_heads, head_dim)
    )
    scores_again = score_of(query_b, key_b)
    probs_again = jnp.exp(scores_again - log_sum)
    prob_grad = jnp.einsum("ihd,jhd->hij", mixed_grad, value_b, preferred_element_type=jnp.float32)
    value_grad = jnp.einsum(
        "hij,ihd->jhd",
        probs_again.astype(jnp.bfloat16),
        mixed_grad,
        preferred_element_type=jnp.float32,
    ).astype(jnp.bfloat16)
    score_grad = probs_again * (prob_grad - jnp.sum(probs_again * prob_grad, -1, keepdims=True))
    grad_rel_bias = jnp.einsum("hij,bij->bh", score_grad, one_hot, precision=highest)
    score_low = score_grad.astype(jnp.bfloat16)
    query_grad = (
        (
            jnp.einsum("hij,jhd->ihd", score_low, key_b, preferred_element_type=jnp.float32)
            * attn_scale
        )
        .astype(jnp.bfloat16)
        .reshape(tok_rows, -1)
    )
    key_grad = (
        (
            jnp.einsum("hij,ihd->jhd", score_low, query_b, preferred_element_type=jnp.float32)
            * attn_scale
        )
        .astype(jnp.bfloat16)
        .reshape(tok_rows, -1)
    )
    value_flat = value_grad.reshape(tok_rows, -1)
    input_part = (
        contract_cols(query_grad, w_query)
        + contract_cols(key_grad, w_key)
        + contract_cols(value_flat, w_value)
    )
    input_grad = sum_over_tp(input_part, 4).astype(jnp.float32)
    grad_gain_attn = jnp.sum(input_grad * normed_a, 0)
    normed_grad_a = input_grad * gain_attn
    grad_inputs = (
        resid_grad
        + scale_a
        * (normed_grad_a - normed_a * jnp.mean(normed_grad_a * normed_a, -1, keepdims=True))
    ).astype(jnp.bfloat16)
    local_width = query_grad.shape[1]
    buckets_count = rel_bias.shape[0]
    flat_bias = grad_rel_bias.reshape(1, -1)
    small_rows = jnp.concatenate(
        [
            grad_gain_attn[None],
            grad_gain_moe[None],
            router_rows,
            jnp.pad(flat_bias, ((0, 0), (0, model_width - flat_bias.shape[1]))),
        ],
        0,
    )
    small_rows = jnp.pad(small_rows, ((0, -small_rows.shape[0] % 16), (0, 0)))
    wide = jnp.concatenate([query_grad, key_grad, value_flat], 1)
    wide = jnp.pad(wide, ((0, 0), (0, -wide.shape[1] % 128)))
    all_wide, all_small = gather_blocks("ex", 5, wide, small_rows.astype(jnp.bfloat16))
    projections = contract_rows(all_attn_in, all_wide.reshape(ex_devices * tok_rows, -1))
    small_sum = jnp.sum(all_small.astype(jnp.float32), 0)
    return (
        output,
        grad_inputs,
        projections[:, :local_width],
        projections[:, local_width : 2 * local_width],
        projections[:, 2 * local_width : 3 * local_width],
        grad_w_attn_out,
        small_sum[0],
        small_sum[1],
        small_sum[2 + experts, : buckets_count * local_heads].reshape(buckets_count, local_heads),
        small_sum[2 : 2 + experts].T,
        grad_w_in,
        grad_w_out,
    )


def solution(mesh):
    placed = (
        P("ex", None),
        P("ex", None),
        P("ex", None),
        P(None, "tp"),
        P(None, "tp"),
        P(None, "tp"),
        P("tp", None),
        P(),
        P(),
        P(None, "tp"),
        P(),
        P("ex", None, "tp"),
        P("ex", "tp", None),
        P("ex", None),
    )
    return jax.shard_map(
        shards,
        mesh=mesh,
        in_specs=placed,
        out_specs=(
            P("ex", None),
            P("ex", None),
            P(None, "tp"),
            P(None, "tp"),
            P(None, "tp"),
            P("tp", None),
            P(),
            P(),
            P(None, "tp"),
            P(),
            P("ex", None, "tp"),
            P("ex", "tp", None),
        ),
        check_vma=False,
    )
```

```python
from functools import partial
import math

import jax
import jax.numpy as jnp
from jax import lax
from jax.experimental import pallas as pl
from jax.experimental.pallas import tpu as pltpu
from jax.sharding import PartitionSpec as P

eps = 1e-06
highest = lax.Precision.HIGHEST
bucket_edges = [math.ceil(16 * 8 ** (number / 16)) for number in range(1, 16)]


def rms_scale(values):
    return lax.rsqrt(jnp.mean(values * values, -1, keepdims=True) + eps)


def bucket_of(length):
    positions = jnp.arange(length, dtype=jnp.int32)
    offsets = positions[:, None] - positions[None, :]
    distance = jnp.maximum(offsets, 0)
    counted = jnp.zeros_like(distance)
    for border in bucket_edges:
        counted = counted + (distance >= border).astype(jnp.int32)
    return jnp.where(distance < 16, distance, 16 + counted)


def contract_rows(left_side, right_side):
    return lax.dot_general(
        left_side, right_side, (((0,), (0,)), ((), ())), preferred_element_type=jnp.float32
    )


def contract_cols(left_side, right_side):
    return lax.dot_general(
        left_side, right_side, (((1,), (1,)), ((), ())), preferred_element_type=jnp.float32
    )


VMEM_BYTES = 48 * 2**20


def flip(index, bit):
    return index + bit * (1 - 2 * ((index // bit) % 2))


def flip_all(index, offset):
    bit = 1
    while bit <= offset:
        if offset & bit:
            index = flip(index, bit)
        bit *= 2
    return index


def bits_of(count):
    bits = []
    bit = count // 2
    while bit:
        bits.append(bit)
        bit //= 2
    return bits


def remote(src, dst, send_sem, recv_sem, axis, peer):
    return pltpu.make_async_remote_copy(
        src_ref=src,
        dst_ref=dst,
        send_sem=send_sem,
        recv_sem=recv_sem,
        device_id={axis: peer},
        device_id_type=pl.DeviceIdType.MESH,
    )


def greet(partners):
    barrier = pltpu.get_barrier_semaphore()
    for axis, peer in partners:
        pl.semaphore_signal(
            barrier, inc=1, device_id={axis: peer}, device_id_type=pl.DeviceIdType.MESH
        )
    pl.semaphore_wait(barrier, len(partners))


def all_peers(axis, count):
    me = lax.axis_index(axis)
    return [(axis, lax.rem(me + step, count)) for step in range(1, count)]


def bit_peers(axis, count):
    me = lax.axis_index(axis)
    return [(axis, flip(me, bit)) for bit in bits_of(count)]


def double_gather(axis, count, sets, sent):
    me = lax.axis_index(axis)
    bits = bits_of(count)

    def send(offset, stage):
        for bit in bits[stage:]:
            for view, send_sems, recv_sems in sets:
                block = view(flip_all(me, offset))
                copy = remote(
                    block,
                    block,
                    send_sems.at[offset ^ bit],
                    recv_sems.at[offset ^ bit],
                    axis,
                    flip(me, bit),
                )
                copy.start()
                sent.append(copy)

    send(0, 0)
    yield
    held = [0]
    for stage, bit in enumerate(bits):
        fresh = []
        for offset in held:
            arrived = offset ^ bit
            for view, send_sems, recv_sems in sets:
                block = view(flip_all(me, arrived))
                remote(
                    block, block, send_sems.at[arrived], recv_sems.at[arrived], axis, flip(me, bit)
                ).wait_recv()
            send(arrived, stage + 1)
            fresh.append(arrived)
        held = held + fresh
        yield


def in_turn(*flows):
    flows = list(flows)
    while flows:
        flows = [flow for flow in flows if next(flow, 1) is None]


def swap_blocks(axis, count, source, target, send_sems, recv_sems, between):
    me = lax.axis_index(axis)
    sent = []
    for step in range(1, count):
        peer = lax.rem(me + step, count)
        copy = remote(
            source(peer), target(me), send_sems.at[step], recv_sems.at[step], axis, peer
        )
        copy.start()
        sent.append(copy)
    between()
    for step in range(1, count):
        origin = lax.rem(me + count - step, count)
        remote(
            source(origin), target(origin), send_sems.at[step], recv_sems.at[step], axis, origin
        ).wait_recv()
    return sent


def finish(sent):
    for copy in sent:
        copy.wait_send()


def sum_kernel(count, ex, number, *refs):
    x_ref, extras = refs[0], refs[1 : 1 + number]
    out_ref, extra_outs = refs[1 + number], refs[2 + number : 2 + 2 * number]
    low_ref, got_ref, s1, r1, s2, r2 = refs[2 + 2 * number : 8 + 2 * number]
    extra_sems = refs[8 + 2 * number :]
    me = lax.axis_index("tp")
    group = lax.axis_index("ex")
    rows = x_ref.shape[0] // count

    def part(ref, index):
        return ref.at[pl.ds(pl.multiple_of(index * rows, rows), rows)]

    low_ref[...] = x_ref[...].astype(jnp.bfloat16)
    sets = []
    for index in range(number):
        extra_out = extra_outs[index]
        extra_out[group] = extras[index][...]
        sets.append(
            (
                lambda i, extra_out=extra_out: extra_out.at[i],
                extra_sems[2 * index],
                extra_sems[2 * index + 1],
            )
        )
    greet(all_peers("tp", count) + bit_peers("ex", ex))
    sent = []
    wide_flow = double_gather("ex", ex, sets, sent)
    first = swap_blocks(
        "tp",
        count,
        lambda i: part(low_ref, i),
        lambda i: got_ref.at[i],
        s1,
        r1,
        lambda: next(wide_flow),
    )
    mine = pl.ds(pl.multiple_of(me * rows, rows), rows)
    got_ref[me] = jnp.zeros(got_ref.shape[1:], jnp.bfloat16)
    total = x_ref[mine, :].astype(jnp.float32)
    for index in range(count):
        total = total + got_ref[index].astype(jnp.float32)
    out_ref[mine, :] = total.astype(jnp.bfloat16)
    in_turn(
        double_gather("tp", count, [(lambda i: part(out_ref, i), s2, r2)], sent), wide_flow
    )
    finish(first + sent)


def dispatch_kernel(ex, tp, x_ref, out_ref, s1, r1, s2, r2):
    me = lax.axis_index("ex")
    column = lax.axis_index("tp")
    bits = bits_of(tp)
    greet(all_peers("ex", ex) + bit_peers("tp", tp))
    out_ref[column, me] = x_ref[me]
    sent = []

    def relay(offset, stage, step, origin):
        for bit in bits[stage:]:
            block = out_ref.at[flip_all(column, offset), origin]
            copy = remote(
                block,
                block,
                s2.at[offset ^ bit, step],
                r2.at[offset ^ bit, step],
                "tp",
                flip(column, bit),
            )
            copy.start()
            sent.append(copy)

    for step in range(1, ex):
        peer = lax.rem(me + step, ex)
        copy = remote(
            x_ref.at[peer], out_ref.at[column, me], s1.at[step], r1.at[step], "ex", peer
        )
        copy.start()
        sent.append(copy)
    for turn in range(ex + 2):
        if turn < ex:
            origin = lax.rem(me + ex - turn, ex)
            if turn:
                remote(
                    x_ref.at[origin],
                    out_ref.at[column, origin],
                    s1.at[turn],
                    r1.at[turn],
                    "ex",
                    origin,
                ).wait_recv()
            relay(0, 0, turn, origin)
        if turn >= 2:
            step = turn - 2
            origin = lax.rem(me + ex - step, ex)
            held = [0]
            for stage, bit in enumerate(bits):
                fresh = [offset ^ bit for offset in held]
                for arrived in fresh:
                    block = out_ref.at[flip_all(column, arrived), origin]
                    remote(
                        block,
                        block,
                        s2.at[arrived, step],
                        r2.at[arrived, step],
                        "tp",
                        flip(column, bit),
                    ).wait_recv()
                    relay(arrived, stage + 1, step, origin)
                held = held + fresh
    finish(sent)


def return_kernel(ex, tp, x_ref, out_ref, held_ref, got_ref, s1, r1, s2, r2):
    me = lax.axis_index("ex")
    column = lax.axis_index("tp")
    greet(all_peers("ex", ex) + bit_peers("tp", tp))
    sent = []
    stages = []
    live = list(range(tp))
    for bit in reversed(bits_of(tp)):
        stages.append((bit, [offset for offset in live if offset & bit]))
        live = [offset for offset in live if not offset & bit]
    steps = list(range(1, ex)) + [0]

    def hop(source, stage, offset, step, target):
        return remote(
            source.at[flip_all(column, offset), target],
            got_ref.at[offset, target],
            s1.at[offset, step],
            r1.at[offset, step],
            "tp",
            flip(column, stages[stage][0]),
        )

    def send(source, stage, step, target):
        for offset in stages[stage][1]:
            copy = hop(source, stage, offset, step, target)
            copy.start()
            sent.append(copy)

    for step in steps:
        send(x_ref, 0, step, lax.rem(me + step, ex))
    source = x_ref
    for stage, (bit, leaving) in enumerate(stages):
        for step in steps:
            target = lax.rem(me + step, ex)
            for offset in leaving:
                hop(source, stage, offset, step, target).wait_recv()
                kept = flip_all(column, offset ^ bit)
                held_ref[kept, target] = (
                    source[kept, target].astype(jnp.float32)
                    + got_ref[offset, target].astype(jnp.float32)
                ).astype(jnp.bfloat16)
            if stage + 1 < len(stages):
                send(held_ref, stage + 1, step, target)
            elif step:
                copy = remote(
                    held_ref.at[column, target],
                    out_ref.at[me],
                    s2.at[step],
                    r2.at[step],
                    "ex",
                    target,
                )
                copy.start()
                sent.append(copy)
            else:
                out_ref[me] = held_ref[column, me]
        source = held_ref
    for step in range(1, ex):
        origin = lax.rem(me + ex - step, ex)
        remote(
            held_ref.at[column, origin], out_ref.at[origin], s2.at[step], r2.at[step], "ex", origin
        ).wait_recv()
    finish(sent)


def gather_kernel(plan, sizes, *refs):
    number = len(plan)
    ins, outs, sems = refs[:number], refs[number : 2 * number], refs[2 * number :]
    axes = sorted(set(axis for axis, _ in plan))
    greet([peer for axis in axes for peer in bit_peers(axis, sizes[axis])])
    sent = []
    flows = []
    for axis in axes:
        me = lax.axis_index(axis)
        sets = []
        for index in range(number):
            if plan[index][0] != axis:
                continue
            out_ref = outs[index]
            if plan[index][1]:
                out_ref[:, me] = ins[index][...]
                view = lambda i, out_ref=out_ref: out_ref.at[:, i]
            else:
                out_ref[me] = ins[index][...]
                view = lambda i, out_ref=out_ref: out_ref.at[i]
            sets.append((view, sems[2 * index], sems[2 * index + 1]))
        flows.append(double_gather(axis, sizes[axis], sets, sent))
    in_turn(*flows)
    finish(sent)


def call_kernel(body, ident, out_shapes, scratch, *operands):
    return pl.pallas_call(
        body,
        out_shape=out_shapes,
        in_specs=[pl.BlockSpec(memory_space=pltpu.VMEM)] * len(operands),
        out_specs=jax.tree.map(lambda _: pl.BlockSpec(memory_space=pltpu.VMEM), out_shapes),
        scratch_shapes=scratch,
        compiler_params=pltpu.CompilerParams(
            collective_id=ident, has_side_effects=True, vmem_limit_bytes=VMEM_BYTES
        ),
    )(*operands)


def sems(*counts):
    return [
        pltpu.SemaphoreType.DMA(count if isinstance(count, tuple) else (count,))
        for count in counts
    ]


def low_shape(*shape):
    return jax.ShapeDtypeStruct(shape, jnp.bfloat16)


def sum_over_tp(ident, values, *extras):
    count, ex = lax.axis_size("tp"), lax.axis_size("ex")
    rows, width = values.shape
    return call_kernel(
        partial(sum_kernel, count, ex, len(extras)),
        ident,
        [low_shape(rows, width)] + [low_shape(ex, *extra.shape) for extra in extras],
        [
            pltpu.VMEM((rows, width), jnp.bfloat16),
            pltpu.VMEM((count, rows // count, width), jnp.bfloat16),
        ]
        + sems(count, count, count, count, *([ex] * (2 * len(extras)))),
        values,
        *extras,
    )


def gather_blocks(ident, plan, *arrays):
    sizes = {axis: lax.axis_size(axis) for axis in ("ex", "tp")}
    shapes = []
    counts = []
    for (axis, inner), array in zip(plan, arrays):
        count = sizes[axis]
        counts += [count, count]
        if inner:
            shapes.append(low_shape(array.shape[0], count, *array.shape[1:]))
        else:
            shapes.append(low_shape(count, *array.shape))
    return call_kernel(
        partial(gather_kernel, plan, sizes), ident, shapes, sems(*counts), *arrays
    )


def shards(
    inputs,
    routes,
    lengths,
    w_query,
    w_key,
    w_value,
    w_attn_out,
    gain_attn,
    gain_moe,
    rel_bias,
    w_router,
    w_in,
    w_out,
    cotangent,
):
    tok_rows, model_width = inputs.shape
    local_heads = rel_bias.shape[1]
    head_dim = w_query.shape[1] // local_heads
    attn_scale = head_dim ** (-0.5)
    experts = w_router.shape[1]
    ex_devices = lax.axis_size("ex")
    local_experts = w_in.shape[0]
    capacity = 4 * tok_rows // experts
    pair_count = 2 * tok_rows
    inputs_f = inputs.astype(jnp.float32)
    scale_a = rms_scale(inputs_f)
    normed_a = inputs_f * scale_a
    attn_in = (normed_a * gain_attn).astype(jnp.bfloat16)
    query_b = (
        jnp.dot(attn_in, w_query, preferred_element_type=jnp.float32)
        .astype(jnp.bfloat16)
        .reshape(tok_rows, local_heads, head_dim)
    )
    key_b = (
        jnp.dot(attn_in, w_key, preferred_element_type=jnp.float32)
        .astype(jnp.bfloat16)
        .reshape(tok_rows, local_heads, head_dim)
    )
    value_b = (
        jnp.dot(attn_in, w_value, preferred_element_type=jnp.float32)
        .astype(jnp.bfloat16)
        .reshape(tok_rows, local_heads, head_dim)
    )
    buckets = bucket_of(tok_rows)
    one_hot = (
        buckets[None] == jnp.arange(rel_bias.shape[0], dtype=jnp.int32)[:, None, None]
    ).astype(jnp.float32)
    bias_full = jnp.einsum("bij,bh->hij", one_hot, rel_bias, precision=highest)
    seq_count = lengths.shape[1]
    seq_order = jnp.arange(seq_count, dtype=jnp.int32)
    seq_ends = jnp.sum(
        jnp.where(seq_order[None, :] <= seq_order[:, None], lengths[0][None, :], 0), -1
    )
    positions = jnp.arange(tok_rows, dtype=jnp.int32)
    segments = jnp.sum((positions[:, None] >= seq_ends[None, :]).astype(jnp.int32), -1)
    allowed = (segments[:, None] == segments[None, :]) & (positions[:, None] >= positions[None, :])

    def score_of(queries_in, keys_in):
        raw_scores = (
            jnp.einsum("ihd,jhd->hij", queries_in, keys_in, preferred_element_type=jnp.float32)
            * attn_scale
        )
        return jnp.where(allowed[None], raw_scores + bias_full, -1e30)

    scores = score_of(query_b, key_b)
    row_max = jnp.max(scores, -1, keepdims=True)
    log_sum = row_max + jnp.log(jnp.sum(jnp.exp(scores - row_max), -1, keepdims=True))
    probabilities = jnp.exp(scores - log_sum)
    probs_low = probabilities.astype(jnp.bfloat16)
    mixed_heads = (
        jnp.einsum("hij,jhd->ihd", probs_low, value_b, preferred_element_type=jnp.float32)
        .astype(jnp.bfloat16)
        .reshape(tok_rows, -1)
    )
    head_part = jnp.dot(mixed_heads, w_attn_out, preferred_element_type=jnp.float32)
    tp_devices = lax.axis_size("tp")
    tp_index = lax.axis_index("tp")
    quarter = tok_rows // tp_devices

    def own_quarter(rows):
        return lax.dynamic_slice_in_dim(rows, tp_index * quarter, quarter, 0)

    head_sum, quarter_in, all_mixed = sum_over_tp(
        0, head_part, own_quarter(attn_in), mixed_heads
    )
    residual = inputs_f + head_sum.astype(jnp.float32)
    scale_m = rms_scale(residual)
    normed_m = residual * scale_m
    moe_in = (normed_m * gain_moe).astype(jnp.bfloat16)
    logits = jnp.dot(moe_in, w_router, preferred_element_type=jnp.float32)
    expert_ids = jnp.arange(experts, dtype=jnp.int32)
    route_hot = (routes[:, :, None] == expert_ids[None, None, :]).astype(jnp.float32)
    chosen_logits = jnp.sum(route_hot * logits[:, None, :], -1)
    gate_max = jnp.max(chosen_logits, -1, keepdims=True)
    gate_exp = jnp.exp(chosen_logits - gate_max)
    gate_values = gate_exp / jnp.sum(gate_exp, -1, keepdims=True)
    pair_routes = routes.reshape(-1)
    pair_hot = (pair_routes[:, None] == expert_ids[None, :]).astype(jnp.int32)
    pair_order = jnp.arange(pair_count, dtype=jnp.int32)
    slot_index = jnp.sum(
        (
            (pair_routes[:, None] == pair_routes[None, :])
            & (pair_order[None, :] < pair_order[:, None])
        ).astype(jnp.int32),
        -1,
    )
    pair_slots = pair_routes * capacity + slot_index
    slot_total = experts * capacity
    pair_cols = pair_slots.reshape(tok_rows, 2).T.reshape(1, pair_count)
    slot_hot = (
        jnp.arange(slot_total, dtype=jnp.int32)[:, None] == pair_cols
    ).astype(jnp.bfloat16)
    grad_out = cotangent.astype(jnp.float32)
    share = 2 * model_width // tp_devices
    half = tp_devices // 2
    moe_pairs = jnp.concatenate([moe_in, moe_in], 0)
    grad_pairs = jnp.concatenate(
        [(gate_values[:, j : j + 1] * grad_out).astype(jnp.bfloat16) for j in range(2)], 0
    )
    pair_rows = lax.dynamic_slice_in_dim(
        jnp.concatenate([moe_pairs, grad_pairs], 1), tp_index * share, share, 1
    )
    send_rows = (
        jnp.dot(slot_hot, pair_rows, preferred_element_type=jnp.float32)
        .astype(jnp.bfloat16)
        .reshape(ex_devices, slot_total // ex_devices, share)
    )
    slots_here = slot_total // ex_devices
    arrived = call_kernel(
        partial(dispatch_kernel, ex_devices, tp_devices),
        1,
        low_shape(tp_devices, ex_devices, slots_here, share),
        sems(ex_devices, ex_devices, *[(tp_devices, ex_devices)] * 2),
        send_rows,
    ).reshape(tp_devices, slot_total, share)
    moe_rows = jnp.concatenate([arrived[i] for i in range(half)], 1)
    grad_rows = jnp.concatenate([arrived[i] for i in range(half, tp_devices)], 1)
    in_here, out_here = w_in[0], w_out[0]
    pre_act = jnp.dot(moe_rows, in_here, preferred_element_type=jnp.float32)
    act_value, gelu_back = jax.vjp(partial(jax.nn.gelu, approximate=True), pre_act)
    act_low = act_value.astype(jnp.bfloat16)
    act_grad = contract_cols(grad_rows, out_here)
    pre_grad = gelu_back(act_grad)[0].astype(jnp.bfloat16)
    partial_out = jnp.dot(act_low, out_here, preferred_element_type=jnp.float32)
    row_part = contract_cols(pre_grad, in_here)
    back_rows = jnp.stack(
        [
            block[:, i * share : (i + 1) * share].astype(jnp.bfloat16)
            for block in (partial_out, row_part)
            for i in range(half)
        ]
    ).reshape(tp_devices, ex_devices, slots_here, share)
    returned = call_kernel(
        partial(return_kernel, ex_devices, tp_devices),
        2,
        low_shape(ex_devices, slots_here, share),
        [
            pltpu.VMEM((tp_devices, ex_devices, slots_here, share), jnp.bfloat16),
            pltpu.VMEM((tp_devices, ex_devices, slots_here, share), jnp.bfloat16),
        ]
        + sems(*[(tp_devices, ex_devices)] * 2, ex_devices, ex_devices),
        back_rows,
    ).reshape(slot_total, share)
    grad_w_out = contract_rows(act_low, grad_rows)[None]
    grad_w_in = contract_rows(moe_rows, pre_grad)[None]
    pair_back = contract_rows(slot_hot, returned)
    is_out = tp_index < half
    weights = jnp.where(is_out, gate_values, 1.0)
    combined = (
        weights[:, 0:1] * pair_back[:tok_rows] + weights[:, 1:2] * pair_back[tok_rows:]
    )
    grad_cols = lax.dynamic_slice_in_dim(grad_out, (tp_index % half) * share, share, 1)
    gate_part = jnp.where(
        is_out,
        jnp.stack(
            [
                jnp.sum(grad_cols * pair_back[:tok_rows], -1),
                jnp.sum(grad_cols * pair_back[tok_rows:], -1),
            ],
            1,
        ),
        0.0,
    )
    gate_high = gate_part.astype(jnp.bfloat16)
    gate_low = (gate_part - gate_high.astype(jnp.float32)).astype(jnp.bfloat16)
    [shared] = gather_blocks(
        3,
        (("tp", False),),
        jnp.concatenate(
            [
                combined.astype(jnp.bfloat16),
                gate_high,
                gate_low,
                jnp.zeros((tok_rows, 124), jnp.bfloat16),
            ],
            1,
        ),
    )
    shared = shared.astype(jnp.float32)
    output = (
        residual + jnp.concatenate([shared[i, :, :share] for i in range(half)], 1)
    ).astype(jnp.bfloat16)
    row_sum = jnp.concatenate([shared[i, :, :share] for i in range(half, tp_devices)], 1)
    gate_grad = jnp.sum(
        shared[:, :, share : share + 2] + shared[:, :, share + 2 : share + 4], 0
    )
    logit_pair = gate_values * (gate_grad - jnp.sum(gate_values * gate_grad, -1, keepdims=True))
    logit_grads = jnp.sum(logit_pair[:, :, None] * route_hot, 1)
    router_rows = jnp.dot(logit_grads.T, moe_in.astype(jnp.float32), precision=highest)
    moe_grad = row_sum + jnp.dot(logit_grads, w_router.astype(jnp.float32).T, precision=highest)
    grad_gain_moe = jnp.sum(moe_grad * normed_m, 0)
    normed_grad_m = moe_grad * gain_moe
    resid_grad = grad_out + scale_m * (
        normed_grad_m - normed_m * jnp.mean(normed_grad_m * normed_m, -1, keepdims=True)
    )
    attn_grad = resid_grad.astype(jnp.bfloat16)
    mixed_grad = (
        contract_cols(attn_grad, w_attn_out)
        .astype(jnp.bfloat16)
        .reshape(tok_rows, local_heads, head_dim)
    )
    scores_again = score_of(query_b, key_b)
    probs_again = jnp.exp(scores_again - log_sum)
    prob_grad = jnp.einsum("ihd,jhd->hij", mixed_grad, value_b, preferred_element_type=jnp.float32)
    value_grad = jnp.einsum(
        "hij,ihd->jhd",
        probs_again.astype(jnp.bfloat16),
        mixed_grad,
        preferred_element_type=jnp.float32,
    ).astype(jnp.bfloat16)
    score_grad = probs_again * (prob_grad - jnp.sum(probs_again * prob_grad, -1, keepdims=True))
    grad_rel_bias = jnp.einsum("hij,bij->bh", score_grad, one_hot, precision=highest)
    score_low = score_grad.astype(jnp.bfloat16)
    query_grad = (
        (
            jnp.einsum("hij,jhd->ihd", score_low, key_b, preferred_element_type=jnp.float32)
            * attn_scale
        )
        .astype(jnp.bfloat16)
        .reshape(tok_rows, -1)
    )
    key_grad = (
        (
            jnp.einsum("hij,ihd->jhd", score_low, query_b, preferred_element_type=jnp.float32)
            * attn_scale
        )
        .astype(jnp.bfloat16)
        .reshape(tok_rows, -1)
    )
    value_flat = value_grad.reshape(tok_rows, -1)
    input_part = (
        contract_cols(query_grad, w_query)
        + contract_cols(key_grad, w_key)
        + contract_cols(value_flat, w_value)
    )
    input_sum, quarter_grad = sum_over_tp(4, input_part, own_quarter(attn_grad))
    input_grad = input_sum.astype(jnp.float32)
    grad_gain_attn = jnp.sum(input_grad * normed_a, 0)
    normed_grad_a = input_grad * gain_attn
    grad_inputs = (
        resid_grad
        + scale_a
        * (normed_grad_a - normed_a * jnp.mean(normed_grad_a * normed_a, -1, keepdims=True))
    ).astype(jnp.bfloat16)
    local_width = query_grad.shape[1]
    buckets_count = rel_bias.shape[0]
    flat_bias = grad_rel_bias.reshape(1, -1)
    small_rows = jnp.concatenate(
        [
            grad_gain_attn[None],
            grad_gain_moe[None],
            router_rows,
            jnp.pad(flat_bias, ((0, 0), (0, model_width - flat_bias.shape[1]))),
        ],
        0,
    )
    small_rows = jnp.pad(small_rows, ((0, -small_rows.shape[0] % 16), (0, 0)))
    wide = jnp.concatenate([query_grad, key_grad, value_flat], 1)
    wide = jnp.pad(wide, ((0, 0), (0, -wide.shape[1] % 128)))
    all_wide, all_small, all_attn_in, all_attn_grad = gather_blocks(
        5,
        (("ex", False), ("ex", False), ("tp", True), ("tp", True)),
        wide,
        small_rows.astype(jnp.bfloat16),
        quarter_in,
        quarter_grad,
    )
    every = ex_devices * tok_rows
    projections = contract_rows(
        all_attn_in.reshape(every, model_width), all_wide.reshape(every, -1)
    )
    grad_w_attn_out = contract_rows(
        all_mixed.reshape(every, -1), all_attn_grad.reshape(every, model_width)
    )
    small_sum = jnp.sum(all_small.astype(jnp.float32), 0)
    return (
        output,
        grad_inputs,
        projections[:, :local_width],
        projections[:, local_width : 2 * local_width],
        projections[:, 2 * local_width : 3 * local_width],
        grad_w_attn_out,
        small_sum[0],
        small_sum[1],
        small_sum[2 + experts, : buckets_count * local_heads].reshape(buckets_count, local_heads),
        small_sum[2 : 2 + experts].T,
        grad_w_in,
        grad_w_out,
    )


def solution(mesh):
    placed = (
        P("ex", None),
        P("ex", None),
        P("ex", None),
        P(None, "tp"),
        P(None, "tp"),
        P(None, "tp"),
        P("tp", None),
        P(),
        P(),
        P(None, "tp"),
        P(),
        P("ex", None, "tp"),
        P("ex", "tp", None),
        P("ex", None),
    )
    return jax.shard_map(
        shards,
        mesh=mesh,
        in_specs=placed,
        out_specs=(
            P("ex", None),
            P("ex", None),
            P(None, "tp"),
            P(None, "tp"),
            P(None, "tp"),
            P("tp", None),
            P(),
            P(),
            P(None, "tp"),
            P(),
            P("ex", None, "tp"),
            P("ex", "tp", None),
        ),
        check_vma=False,
    )
```

```python
from functools import partial
import math

import jax
import jax.numpy as jnp
from jax import lax
from jax.experimental import pallas as pl
from jax.experimental.pallas import tpu as pltpu
from jax.sharding import PartitionSpec as P

eps = 1e-06
highest = lax.Precision.HIGHEST
bucket_edges = [math.ceil(16 * 8 ** (number / 16)) for number in range(1, 16)]


def rms_scale(values):
    return lax.rsqrt(jnp.mean(values * values, -1, keepdims=True) + eps)


def bucket_of(length):
    positions = jnp.arange(length, dtype=jnp.int32)
    offsets = positions[:, None] - positions[None, :]
    distance = jnp.maximum(offsets, 0)
    counted = jnp.zeros_like(distance)
    for border in bucket_edges:
        counted = counted + (distance >= border).astype(jnp.int32)
    return jnp.where(distance < 16, distance, 16 + counted)


def contract_rows(left_side, right_side):
    return lax.dot_general(
        left_side, right_side, (((0,), (0,)), ((), ())), preferred_element_type=jnp.float32
    )


def contract_cols(left_side, right_side):
    return lax.dot_general(
        left_side, right_side, (((1,), (1,)), ((), ())), preferred_element_type=jnp.float32
    )


VMEM_BYTES = 48 * 2**20


def flip(index, bit):
    return index + bit * (1 - 2 * ((index // bit) % 2))


def flip_all(index, offset):
    bit = 1
    while bit <= offset:
        if offset & bit:
            index = flip(index, bit)
        bit *= 2
    return index


def bits_of(count):
    bits = []
    bit = count // 2
    while bit:
        bits.append(bit)
        bit //= 2
    return bits


def remote(src, dst, send_sem, recv_sem, axis, peer):
    return pltpu.make_async_remote_copy(
        src_ref=src,
        dst_ref=dst,
        send_sem=send_sem,
        recv_sem=recv_sem,
        device_id={axis: peer},
        device_id_type=pl.DeviceIdType.MESH,
    )


def greet(partners):
    barrier = pltpu.get_barrier_semaphore()
    for axis, peer in partners:
        pl.semaphore_signal(
            barrier, inc=1, device_id={axis: peer}, device_id_type=pl.DeviceIdType.MESH
        )
    pl.semaphore_wait(barrier, len(partners))


def all_peers(axis, count):
    me = lax.axis_index(axis)
    return [(axis, lax.rem(me + step, count)) for step in range(1, count)]


def bit_peers(axis, count):
    me = lax.axis_index(axis)
    return [(axis, flip(me, bit)) for bit in bits_of(count)]


def double_gather(axis, count, sets, sent):
    me = lax.axis_index(axis)
    bits = bits_of(count)

    def send(offset, stage):
        for bit in bits[stage:]:
            for view, send_sems, recv_sems in sets:
                block = view(flip_all(me, offset))
                copy = remote(
                    block,
                    block,
                    send_sems.at[offset ^ bit],
                    recv_sems.at[offset ^ bit],
                    axis,
                    flip(me, bit),
                )
                copy.start()
                sent.append(copy)

    send(0, 0)
    yield
    held = [0]
    for stage, bit in enumerate(bits):
        fresh = []
        for offset in held:
            arrived = offset ^ bit
            for view, send_sems, recv_sems in sets:
                block = view(flip_all(me, arrived))
                remote(
                    block, block, send_sems.at[arrived], recv_sems.at[arrived], axis, flip(me, bit)
                ).wait_recv()
            send(arrived, stage + 1)
            fresh.append(arrived)
        held = held + fresh
        yield


def in_turn(*flows):
    flows = list(flows)
    while flows:
        flows = [flow for flow in flows if next(flow, 1) is None]


def swap_blocks(axis, count, source, target, send_sems, recv_sems, between):
    me = lax.axis_index(axis)
    sent = []
    for step in range(1, count):
        peer = lax.rem(me + step, count)
        copy = remote(
            source(peer), target(me), send_sems.at[step], recv_sems.at[step], axis, peer
        )
        copy.start()
        sent.append(copy)
    between()
    for step in range(1, count):
        origin = lax.rem(me + count - step, count)
        remote(
            source(origin), target(origin), send_sems.at[step], recv_sems.at[step], axis, origin
        ).wait_recv()
    return sent


def finish(sent):
    for copy in sent:
        copy.wait_send()


def sum_kernel(count, ex, number, *refs):
    x_ref, extras = refs[0], refs[1 : 1 + number]
    out_ref, extra_outs = refs[1 + number], refs[2 + number : 2 + 2 * number]
    low_ref, got_ref, s1, r1, s2, r2 = refs[2 + 2 * number : 8 + 2 * number]
    extra_sems = refs[8 + 2 * number :]
    me = lax.axis_index("tp")
    group = lax.axis_index("ex")
    rows = x_ref.shape[0] // count

    def part(ref, index):
        return ref.at[pl.ds(pl.multiple_of(index * rows, rows), rows)]

    low_ref[...] = x_ref[...].astype(jnp.bfloat16)
    sets = []
    for index in range(number):
        extra_out = extra_outs[index]
        extra_out[group] = extras[index][...]
        sets.append(
            (
                lambda i, extra_out=extra_out: extra_out.at[i],
                extra_sems[2 * index],
                extra_sems[2 * index + 1],
            )
        )
    greet(all_peers("tp", count) + bit_peers("ex", ex))
    sent = []
    wide_flow = double_gather("ex", ex, sets, sent)
    first = swap_blocks(
        "tp",
        count,
        lambda i: part(low_ref, i),
        lambda i: got_ref.at[i],
        s1,
        r1,
        lambda: next(wide_flow),
    )
    mine = pl.ds(pl.multiple_of(me * rows, rows), rows)
    got_ref[me] = jnp.zeros(got_ref.shape[1:], jnp.bfloat16)
    total = x_ref[mine, :].astype(jnp.float32)
    for index in range(count):
        total = total + got_ref[index].astype(jnp.float32)
    out_ref[mine, :] = total.astype(jnp.bfloat16)
    in_turn(
        double_gather("tp", count, [(lambda i: part(out_ref, i), s2, r2)], sent), wide_flow
    )
    finish(first + sent)


def dispatch_kernel(ex, tp, x_ref, out_ref, s1, r1, s2, r2):
    me = lax.axis_index("ex")
    column = lax.axis_index("tp")
    bits = bits_of(tp)
    greet(all_peers("ex", ex) + bit_peers("tp", tp))
    out_ref[column, me] = x_ref[me]
    sent = []

    def relay(offset, stage, step, origin):
        for bit in bits[stage:]:
            block = out_ref.at[flip_all(column, offset), origin]
            copy = remote(
                block,
                block,
                s2.at[offset ^ bit, step],
                r2.at[offset ^ bit, step],
                "tp",
                flip(column, bit),
            )
            copy.start()
            sent.append(copy)

    for step in range(1, ex):
        peer = lax.rem(me + step, ex)
        copy = remote(
            x_ref.at[peer], out_ref.at[column, me], s1.at[step], r1.at[step], "ex", peer
        )
        copy.start()
        sent.append(copy)
    for turn in range(ex + 2):
        if turn < ex:
            origin = lax.rem(me + ex - turn, ex)
            if turn:
                remote(
                    x_ref.at[origin],
                    out_ref.at[column, origin],
                    s1.at[turn],
                    r1.at[turn],
                    "ex",
                    origin,
                ).wait_recv()
            relay(0, 0, turn, origin)
        if turn >= 2:
            step = turn - 2
            origin = lax.rem(me + ex - step, ex)
            held = [0]
            for stage, bit in enumerate(bits):
                fresh = [offset ^ bit for offset in held]
                for arrived in fresh:
                    block = out_ref.at[flip_all(column, arrived), origin]
                    remote(
                        block,
                        block,
                        s2.at[arrived, step],
                        r2.at[arrived, step],
                        "tp",
                        flip(column, bit),
                    ).wait_recv()
                    relay(arrived, stage + 1, step, origin)
                held = held + fresh
    finish(sent)


def return_kernel(ex, tp, x_ref, out_ref, held_ref, got_ref, s1, r1, s2, r2):
    me = lax.axis_index("ex")
    column = lax.axis_index("tp")
    greet(all_peers("ex", ex) + bit_peers("tp", tp))
    sent = []
    stages = []
    live = list(range(tp))
    for bit in reversed(bits_of(tp)):
        stages.append((bit, [offset for offset in live if offset & bit]))
        live = [offset for offset in live if not offset & bit]
    steps = list(range(1, ex)) + [0]

    def hop(source, stage, offset, step, target):
        return remote(
            source.at[flip_all(column, offset), target],
            got_ref.at[offset, target],
            s1.at[offset, step],
            r1.at[offset, step],
            "tp",
            flip(column, stages[stage][0]),
        )

    def send(source, stage, step, target):
        for offset in stages[stage][1]:
            copy = hop(source, stage, offset, step, target)
            copy.start()
            sent.append(copy)

    for step in steps:
        send(x_ref, 0, step, lax.rem(me + step, ex))
    source = x_ref
    for stage, (bit, leaving) in enumerate(stages):
        for step in steps:
            target = lax.rem(me + step, ex)
            for offset in leaving:
                hop(source, stage, offset, step, target).wait_recv()
                kept = flip_all(column, offset ^ bit)
                held_ref[kept, target] = (
                    source[kept, target].astype(jnp.float32)
                    + got_ref[offset, target].astype(jnp.float32)
                ).astype(jnp.bfloat16)
            if stage + 1 < len(stages):
                send(held_ref, stage + 1, step, target)
            elif step:
                copy = remote(
                    held_ref.at[column, target],
                    out_ref.at[me],
                    s2.at[step],
                    r2.at[step],
                    "ex",
                    target,
                )
                copy.start()
                sent.append(copy)
            else:
                out_ref[me] = held_ref[column, me]
        source = held_ref
    for step in range(1, ex):
        origin = lax.rem(me + ex - step, ex)
        remote(
            held_ref.at[column, origin], out_ref.at[origin], s2.at[step], r2.at[step], "ex", origin
        ).wait_recv()
    finish(sent)


def gather_kernel(plan, sizes, *refs):
    number = len(plan)
    ins, outs, sems = refs[:number], refs[number : 2 * number], refs[2 * number :]
    axes = sorted(set(axis for axis, _ in plan))
    greet([peer for axis in axes for peer in bit_peers(axis, sizes[axis])])
    sent = []
    flows = []
    for axis in axes:
        me = lax.axis_index(axis)
        sets = []
        for index in range(number):
            if plan[index][0] != axis:
                continue
            out_ref = outs[index]
            if plan[index][1]:
                out_ref[:, me] = ins[index][...]
                view = lambda i, out_ref=out_ref: out_ref.at[:, i]
            else:
                out_ref[me] = ins[index][...]
                view = lambda i, out_ref=out_ref: out_ref.at[i]
            sets.append((view, sems[2 * index], sems[2 * index + 1]))
        flows.append(double_gather(axis, sizes[axis], sets, sent))
    in_turn(*flows)
    finish(sent)


def call_kernel(body, ident, out_shapes, scratch, *operands):
    return pl.pallas_call(
        body,
        out_shape=out_shapes,
        in_specs=[pl.BlockSpec(memory_space=pltpu.VMEM)] * len(operands),
        out_specs=jax.tree.map(lambda _: pl.BlockSpec(memory_space=pltpu.VMEM), out_shapes),
        scratch_shapes=scratch,
        compiler_params=pltpu.CompilerParams(
            collective_id=ident, has_side_effects=True, vmem_limit_bytes=VMEM_BYTES
        ),
    )(*operands)


def sems(*counts):
    return [
        pltpu.SemaphoreType.DMA(count if isinstance(count, tuple) else (count,))
        for count in counts
    ]


def low_shape(*shape):
    return jax.ShapeDtypeStruct(shape, jnp.bfloat16)


def sum_over_tp(ident, values, *extras):
    count, ex = lax.axis_size("tp"), lax.axis_size("ex")
    rows, width = values.shape
    return call_kernel(
        partial(sum_kernel, count, ex, len(extras)),
        ident,
        [low_shape(rows, width)] + [low_shape(ex, *extra.shape) for extra in extras],
        [
            pltpu.VMEM((rows, width), jnp.bfloat16),
            pltpu.VMEM((count, rows // count, width), jnp.bfloat16),
        ]
        + sems(count, count, count, count, *([ex] * (2 * len(extras)))),
        values,
        *extras,
    )


def gather_blocks(ident, plan, *arrays):
    sizes = {axis: lax.axis_size(axis) for axis in ("ex", "tp")}
    shapes = []
    counts = []
    for (axis, inner), array in zip(plan, arrays):
        count = sizes[axis]
        counts += [count, count]
        if inner:
            shapes.append(low_shape(array.shape[0], count, *array.shape[1:]))
        else:
            shapes.append(low_shape(count, *array.shape))
    return call_kernel(
        partial(gather_kernel, plan, sizes), ident, shapes, sems(*counts), *arrays
    )


def shards(
    inputs,
    routes,
    lengths,
    w_query,
    w_key,
    w_value,
    w_attn_out,
    gain_attn,
    gain_moe,
    rel_bias,
    w_router,
    w_in,
    w_out,
    cotangent,
):
    tok_rows, model_width = inputs.shape
    local_heads = rel_bias.shape[1]
    head_dim = w_query.shape[1] // local_heads
    attn_scale = head_dim ** (-0.5)
    experts = w_router.shape[1]
    ex_devices = lax.axis_size("ex")
    local_experts = w_in.shape[0]
    capacity = 4 * tok_rows // experts
    pair_count = 2 * tok_rows
    inputs_f = inputs.astype(jnp.float32)
    scale_a = rms_scale(inputs_f)
    normed_a = inputs_f * scale_a
    attn_in = (normed_a * gain_attn).astype(jnp.bfloat16)
    query_b = (
        jnp.dot(attn_in, w_query, preferred_element_type=jnp.float32)
        .astype(jnp.bfloat16)
        .reshape(tok_rows, local_heads, head_dim)
    )
    key_b = (
        jnp.dot(attn_in, w_key, preferred_element_type=jnp.float32)
        .astype(jnp.bfloat16)
        .reshape(tok_rows, local_heads, head_dim)
    )
    value_b = (
        jnp.dot(attn_in, w_value, preferred_element_type=jnp.float32)
        .astype(jnp.bfloat16)
        .reshape(tok_rows, local_heads, head_dim)
    )
    buckets = bucket_of(tok_rows)
    one_hot = (
        buckets[None] == jnp.arange(rel_bias.shape[0], dtype=jnp.int32)[:, None, None]
    ).astype(jnp.float32)
    bias_full = jnp.einsum("bij,bh->hij", one_hot, rel_bias, precision=highest)
    seq_count = lengths.shape[1]
    seq_order = jnp.arange(seq_count, dtype=jnp.int32)
    seq_ends = jnp.sum(
        jnp.where(seq_order[None, :] <= seq_order[:, None], lengths[0][None, :], 0), -1
    )
    positions = jnp.arange(tok_rows, dtype=jnp.int32)
    segments = jnp.sum((positions[:, None] >= seq_ends[None, :]).astype(jnp.int32), -1)
    allowed = (segments[:, None] == segments[None, :]) & (positions[:, None] >= positions[None, :])

    def score_of(queries_in, keys_in):
        raw_scores = (
            jnp.einsum("ihd,jhd->hij", queries_in, keys_in, preferred_element_type=jnp.float32)
            * attn_scale
        )
        return jnp.where(allowed[None], raw_scores + bias_full, -1e30)

    scores = score_of(query_b, key_b)
    row_max = jnp.max(scores, -1, keepdims=True)
    log_sum = row_max + jnp.log(jnp.sum(jnp.exp(scores - row_max), -1, keepdims=True))
    probabilities = jnp.exp(scores - log_sum)
    probs_low = probabilities.astype(jnp.bfloat16)
    mixed_heads = (
        jnp.einsum("hij,jhd->ihd", probs_low, value_b, preferred_element_type=jnp.float32)
        .astype(jnp.bfloat16)
        .reshape(tok_rows, -1)
    )
    head_part = jnp.dot(mixed_heads, w_attn_out, preferred_element_type=jnp.float32)
    tp_devices = lax.axis_size("tp")
    tp_index = lax.axis_index("tp")
    quarter = tok_rows // tp_devices

    def own_quarter(rows):
        return lax.dynamic_slice_in_dim(rows, tp_index * quarter, quarter, 0)

    mixed_width = mixed_heads.shape[1]
    early_rows = lax.all_gather(
        jnp.concatenate(
            [attn_in, jnp.pad(mixed_heads, ((0, 0), (0, -mixed_width % 128)))], 1
        ),
        "ex",
        axis=0,
        tiled=True,
    )
    [head_sum] = sum_over_tp(0, head_part)
    residual = inputs_f + head_sum.astype(jnp.float32)
    scale_m = rms_scale(residual)
    normed_m = residual * scale_m
    moe_in = (normed_m * gain_moe).astype(jnp.bfloat16)
    logits = jnp.dot(moe_in, w_router, preferred_element_type=jnp.float32)
    expert_ids = jnp.arange(experts, dtype=jnp.int32)
    route_hot = (routes[:, :, None] == expert_ids[None, None, :]).astype(jnp.float32)
    chosen_logits = jnp.sum(route_hot * logits[:, None, :], -1)
    gate_max = jnp.max(chosen_logits, -1, keepdims=True)
    gate_exp = jnp.exp(chosen_logits - gate_max)
    gate_values = gate_exp / jnp.sum(gate_exp, -1, keepdims=True)
    pair_routes = routes.reshape(-1)
    pair_hot = (pair_routes[:, None] == expert_ids[None, :]).astype(jnp.int32)
    pair_order = jnp.arange(pair_count, dtype=jnp.int32)
    slot_index = jnp.sum(
        (
            (pair_routes[:, None] == pair_routes[None, :])
            & (pair_order[None, :] < pair_order[:, None])
        ).astype(jnp.int32),
        -1,
    )
    pair_slots = pair_routes * capacity + slot_index
    slot_total = experts * capacity
    pair_cols = pair_slots.reshape(tok_rows, 2).T.reshape(1, pair_count)
    slot_hot = (
        jnp.arange(slot_total, dtype=jnp.int32)[:, None] == pair_cols
    ).astype(jnp.bfloat16)
    grad_out = cotangent.astype(jnp.float32)
    share = 2 * model_width // tp_devices
    half = tp_devices // 2
    moe_pairs = jnp.concatenate([moe_in, moe_in], 0)
    grad_pairs = jnp.concatenate(
        [(gate_values[:, j : j + 1] * grad_out).astype(jnp.bfloat16) for j in range(2)], 0
    )
    pair_rows = lax.dynamic_slice_in_dim(
        jnp.concatenate([moe_pairs, grad_pairs], 1), tp_index * share, share, 1
    )
    send_rows = (
        jnp.dot(slot_hot, pair_rows, preferred_element_type=jnp.float32)
        .astype(jnp.bfloat16)
        .reshape(ex_devices, slot_total // ex_devices, share)
    )
    slots_here = slot_total // ex_devices
    arrived = call_kernel(
        partial(dispatch_kernel, ex_devices, tp_devices),
        1,
        low_shape(tp_devices, ex_devices, slots_here, share),
        sems(ex_devices, ex_devices, *[(tp_devices, ex_devices)] * 2),
        send_rows,
    ).reshape(tp_devices, slot_total, share)
    moe_rows = jnp.concatenate([arrived[i] for i in range(half)], 1)
    grad_rows = jnp.concatenate([arrived[i] for i in range(half, tp_devices)], 1)
    in_here, out_here = w_in[0], w_out[0]
    pre_act = jnp.dot(moe_rows, in_here, preferred_element_type=jnp.float32)
    act_value, gelu_back = jax.vjp(partial(jax.nn.gelu, approximate=True), pre_act)
    act_low = act_value.astype(jnp.bfloat16)
    act_grad = contract_cols(grad_rows, out_here)
    pre_grad = gelu_back(act_grad)[0].astype(jnp.bfloat16)
    partial_out = jnp.dot(act_low, out_here, preferred_element_type=jnp.float32)
    row_part = contract_cols(pre_grad, in_here)
    back_rows = jnp.stack(
        [
            block[:, i * share : (i + 1) * share].astype(jnp.bfloat16)
            for block in (partial_out, row_part)
            for i in range(half)
        ]
    ).reshape(tp_devices, ex_devices, slots_here, share)
    returned = call_kernel(
        partial(return_kernel, ex_devices, tp_devices),
        2,
        low_shape(ex_devices, slots_here, share),
        [
            pltpu.VMEM((tp_devices, ex_devices, slots_here, share), jnp.bfloat16),
            pltpu.VMEM((tp_devices, ex_devices, slots_here, share), jnp.bfloat16),
        ]
        + sems(*[(tp_devices, ex_devices)] * 2, ex_devices, ex_devices),
        back_rows,
    ).reshape(slot_total, share)
    grad_w_out = contract_rows(act_low, grad_rows)[None]
    grad_w_in = contract_rows(moe_rows, pre_grad)[None]
    pair_back = contract_rows(slot_hot, returned)
    is_out = tp_index < half
    weights = jnp.where(is_out, gate_values, 1.0)
    combined = (
        weights[:, 0:1] * pair_back[:tok_rows] + weights[:, 1:2] * pair_back[tok_rows:]
    )
    grad_cols = lax.dynamic_slice_in_dim(grad_out, (tp_index % half) * share, share, 1)
    gate_part = jnp.where(
        is_out,
        jnp.stack(
            [
                jnp.sum(grad_cols * pair_back[:tok_rows], -1),
                jnp.sum(grad_cols * pair_back[tok_rows:], -1),
            ],
            1,
        ),
        0.0,
    )
    gate_high = gate_part.astype(jnp.bfloat16)
    gate_low = (gate_part - gate_high.astype(jnp.float32)).astype(jnp.bfloat16)
    [shared] = gather_blocks(
        3,
        (("tp", False),),
        jnp.concatenate(
            [
                combined.astype(jnp.bfloat16),
                gate_high,
                gate_low,
                jnp.zeros((tok_rows, 124), jnp.bfloat16),
            ],
            1,
        ),
    )
    shared = shared.astype(jnp.float32)
    output = (
        residual + jnp.concatenate([shared[i, :, :share] for i in range(half)], 1)
    ).astype(jnp.bfloat16)
    row_sum = jnp.concatenate([shared[i, :, :share] for i in range(half, tp_devices)], 1)
    gate_grad = jnp.sum(
        shared[:, :, share : share + 2] + shared[:, :, share + 2 : share + 4], 0
    )
    logit_pair = gate_values * (gate_grad - jnp.sum(gate_values * gate_grad, -1, keepdims=True))
    logit_grads = jnp.sum(logit_pair[:, :, None] * route_hot, 1)
    router_rows = jnp.dot(logit_grads.T, moe_in.astype(jnp.float32), precision=highest)
    moe_grad = row_sum + jnp.dot(logit_grads, w_router.astype(jnp.float32).T, precision=highest)
    grad_gain_moe = jnp.sum(moe_grad * normed_m, 0)
    normed_grad_m = moe_grad * gain_moe
    resid_grad = grad_out + scale_m * (
        normed_grad_m - normed_m * jnp.mean(normed_grad_m * normed_m, -1, keepdims=True)
    )
    attn_grad = resid_grad.astype(jnp.bfloat16)
    mixed_grad = (
        contract_cols(attn_grad, w_attn_out)
        .astype(jnp.bfloat16)
        .reshape(tok_rows, local_heads, head_dim)
    )
    scores_again = score_of(query_b, key_b)
    probs_again = jnp.exp(scores_again - log_sum)
    prob_grad = jnp.einsum("ihd,jhd->hij", mixed_grad, value_b, preferred_element_type=jnp.float32)
    value_grad = jnp.einsum(
        "hij,ihd->jhd",
        probs_again.astype(jnp.bfloat16),
        mixed_grad,
        preferred_element_type=jnp.float32,
    ).astype(jnp.bfloat16)
    score_grad = probs_again * (prob_grad - jnp.sum(probs_again * prob_grad, -1, keepdims=True))
    grad_rel_bias = jnp.einsum("hij,bij->bh", score_grad, one_hot, precision=highest)
    score_low = score_grad.astype(jnp.bfloat16)
    query_grad = (
        (
            jnp.einsum("hij,jhd->ihd", score_low, key_b, preferred_element_type=jnp.float32)
            * attn_scale
        )
        .astype(jnp.bfloat16)
        .reshape(tok_rows, -1)
    )
    key_grad = (
        (
            jnp.einsum("hij,ihd->jhd", score_low, query_b, preferred_element_type=jnp.float32)
            * attn_scale
        )
        .astype(jnp.bfloat16)
        .reshape(tok_rows, -1)
    )
    value_flat = value_grad.reshape(tok_rows, -1)
    input_part = (
        contract_cols(query_grad, w_query)
        + contract_cols(key_grad, w_key)
        + contract_cols(value_flat, w_value)
    )
    input_sum, quarter_grad = sum_over_tp(4, input_part, own_quarter(attn_grad))
    input_grad = input_sum.astype(jnp.float32)
    grad_gain_attn = jnp.sum(input_grad * normed_a, 0)
    normed_grad_a = input_grad * gain_attn
    grad_inputs = (
        resid_grad
        + scale_a
        * (normed_grad_a - normed_a * jnp.mean(normed_grad_a * normed_a, -1, keepdims=True))
    ).astype(jnp.bfloat16)
    local_width = query_grad.shape[1]
    buckets_count = rel_bias.shape[0]
    flat_bias = grad_rel_bias.reshape(1, -1)
    small_rows = jnp.concatenate(
        [
            grad_gain_attn[None],
            grad_gain_moe[None],
            router_rows,
            jnp.pad(flat_bias, ((0, 0), (0, model_width - flat_bias.shape[1]))),
        ],
        0,
    )
    small_rows = jnp.pad(small_rows, ((0, -small_rows.shape[0] % 16), (0, 0)))
    wide = jnp.concatenate([query_grad, key_grad, value_flat], 1)
    wide = jnp.pad(wide, ((0, 0), (0, -wide.shape[1] % 128)))
    all_wide, all_small, all_attn_grad = gather_blocks(
        5,
        (("ex", False), ("ex", False), ("tp", True)),
        wide,
        small_rows.astype(jnp.bfloat16),
        quarter_grad,
    )
    every = ex_devices * tok_rows
    projections = contract_rows(
        early_rows[:, :model_width], all_wide.reshape(every, -1)
    )
    grad_w_attn_out = contract_rows(
        early_rows[:, model_width : model_width + mixed_width], all_attn_grad.reshape(every, model_width)
    )
    small_sum = jnp.sum(all_small.astype(jnp.float32), 0)
    return (
        output,
        grad_inputs,
        projections[:, :local_width],
        projections[:, local_width : 2 * local_width],
        projections[:, 2 * local_width : 3 * local_width],
        grad_w_attn_out,
        small_sum[0],
        small_sum[1],
        small_sum[2 + experts, : buckets_count * local_heads].reshape(buckets_count, local_heads),
        small_sum[2 : 2 + experts].T,
        grad_w_in,
        grad_w_out,
    )


def solution(mesh):
    placed = (
        P("ex", None),
        P("ex", None),
        P("ex", None),
        P(None, "tp"),
        P(None, "tp"),
        P(None, "tp"),
        P("tp", None),
        P(),
        P(),
        P(None, "tp"),
        P(),
        P("ex", None, "tp"),
        P("ex", "tp", None),
        P("ex", None),
    )
    return jax.shard_map(
        shards,
        mesh=mesh,
        in_specs=placed,
        out_specs=(
            P("ex", None),
            P("ex", None),
            P(None, "tp"),
            P(None, "tp"),
            P(None, "tp"),
            P("tp", None),
            P(),
            P(),
            P(None, "tp"),
            P(),
            P("ex", None, "tp"),
            P("ex", "tp", None),
        ),
        check_vma=False,
    )
```
